256 devices in a mesh: dp: 16 (over z, y_lo), fsdp: 16 (over y_hi, x, core).
Axes of the slice: x: 4, y: 4 (y_hi: 2, y_lo: 2; y = y_hi * 2 + y_lo), z: 8, core: 2. Of those that a mesh axis runs over, the one named last changes fastest.
Arguments:
- tokens_in: bfloat16 [32768, 2560], P(('dp', 'fsdp')), may hold values from -6 to 6
- queries_first: bfloat16 [32768, 2560], P(('dp', 'fsdp')), may hold values from -6 to 6
- queries_second: bfloat16 [32768, 2560], P(('dp', 'fsdp')), may hold values from -6 to 6
- teacher_logits: bfloat16 [32768, 256], P(('dp', 'fsdp')), may hold values from -15 to 15
- rollout_lengths: int32 [16, 16, 32], P(None, 'fsdp'), may hold values from 1 to 12, as said below
- send_counts: int32 [16, 16, 16], P(None, 'fsdp'), may hold values from 1 to 3, as said below
- key_value_weight: bfloat16 [2560, 1024], P('fsdp'), may hold values from -0.125 to 0.125
- head_slice: bfloat16 [2560, 256], P('fsdp'), may hold values from -0.375 to 0.375
Outputs:
- input_grad: bfloat16 [32768, 2560], P(('dp', 'fsdp'))
- kv_grad: float32 [2560, 1024], P('fsdp')
- head_grad: float32 [2560, 256], P('fsdp')
The draws below stay inside these ranges and needn't reach their ends.
Inputs may be any that keep to these rules, and one draw needn't show every extreme that they name: `rollout_lengths`: each device's rollout lengths sum to 128. The rollouts that one device sends to one group span at most 12 rows, exactly 12 for some group, and every device (d, f) receives exactly 128 rows in all. `send_counts`: for every device the counts sum to 32.
All inputs are finite; a program needn't handle non-finite values.
Results may differ from the reference program's by a relative error of at most 0.025.
Values may be sent and summed in bfloat16 or wider, within the bound.
A program may use at most 128 MiB of HBM per device.

```python
import jax
import jax.numpy as jnp
from jax import lax

MODEL_WIDTH = 2560
KEY_VALUE_HEADS = 4
HEADS_PER_KEY = 5
HEAD_SIZE = 128
VOCAB_SLICE = 256
TOK_DEV = 128
NR = 32
TOKENS = 32768
N_DP = 16
N_FSDP = 16


def permute_groups(group_key):
    return jax.random.permutation(group_key, N_DP)


def rollout_plan(key):
    half = TOK_DEV // (2 * N_DP)
    mean_rows = TOK_DEV // N_DP
    pairs = N_DP // 2
    subkeys = jax.random.split(key, 6)
    delta = jax.random.randint(subkeys[0], (N_FSDP, pairs), 0, half + 1)
    delta = delta.at[:, 0].set(half)
    pattern = jax.random.randint(subkeys[1], (N_FSDP, pairs), 0, 3)
    pattern = pattern.at[:, 0].set(1)
    first_count = jnp.where(pattern == 0, 2, jnp.where(pattern == 1, 1, 3))
    base_rows = jnp.stack([mean_rows + delta, mean_rows - delta], -1).reshape(N_FSDP, N_DP)
    base_count = jnp.stack([first_count, 4 - first_count], -1).reshape(N_FSDP, N_DP)
    shuffle = jax.vmap(permute_groups)(jax.random.split(subkeys[2], N_FSDP))
    base_rows = jnp.take_along_axis(base_rows, shuffle, 1)
    base_count = jnp.take_along_axis(base_count, shuffle, 1)
    sigma = jax.vmap(permute_groups)(jax.random.split(subkeys[3], N_FSDP))
    group = jnp.arange(N_DP)
    slot = (sigma[None, :, :] - group[:, None, None]) % N_DP
    fsdp_index = jnp.arange(N_FSDP)[None, :, None]
    packed_row_list = base_rows[fsdp_index, slot]
    count = base_count[fsdp_index, slot]
    cut_one = jax.random.randint(subkeys[4], packed_row_list.shape, 1, packed_row_list - jnp.maximum(count - 2, 0))
    cut_two = jax.random.randint(subkeys[5], packed_row_list.shape, cut_one + 1, jnp.maximum(packed_row_list, cut_one + 2))
    part_one = jnp.where(count == 1, packed_row_list, cut_one)
    part_two = jnp.where(count == 1, 0, jnp.where(count == 2, packed_row_list - cut_one, cut_two - cut_one))
    part_three = jnp.where(count == 3, packed_row_list - cut_two, 0)
    parts = jnp.stack([part_one, part_two, part_three], -1).reshape(N_DP, N_FSDP, 3 * N_DP)
    order = jnp.argsort((parts == 0).astype(jnp.int32), axis=-1, stable=True)
    lengths = jnp.take_along_axis(parts, order, -1)[..., :2 * N_DP]
    return (lengths.astype(jnp.int32), count.astype(jnp.int32))


def draw_rollout_lengths(key, part):
    plan = rollout_plan(key)
    return plan[0]


def draw_send_counts(key, part):
    plan = rollout_plan(key)
    return plan[1]


def shard_levels(own_key, shape, cuts, smallest, high):
    loudness, own = 1.0, jax.random.fold_in(own_key, 6)
    for axis_at, shards_of in cuts:
        heights = jnp.exp(jax.random.uniform(jax.random.fold_in(own, axis_at), (shards_of,), jnp.float32, smallest / len(cuts), high / len(cuts)))
        loudness = loudness * jnp.repeat(heights, shape[axis_at] // shards_of).reshape([-1 if axis == axis_at else 1 for axis in range(len(shape))])
    return loudness


def gaussian(own_key, shape, scale, bound, pieces=(), kind=jnp.bfloat16):
    result = scale * jax.random.normal(own_key, shape, jnp.float32)
    if pieces:
        result = result * shard_levels(own_key, shape, pieces, -0.22, 0.18)
    return jnp.clip(result, -bound, bound).astype(kind)


def setup_inputs(seed: int = 0) -> dict:
    seeds = jax.random.split(jax.random.key(seed), 9)
    return {
        "tokens_in": gaussian(seeds[0], (TOKENS, MODEL_WIDTH), 1.0, 6.0, ((0, 256),)),
        "queries_first": gaussian(seeds[1], (TOKENS, MODEL_WIDTH), 1.0, 6.0, ((0, 256),)),
        "queries_second": gaussian(seeds[2], (TOKENS, MODEL_WIDTH), 1.0, 6.0, ((0, 256),)),
        "teacher_logits": gaussian(seeds[3], (TOKENS, VOCAB_SLICE), 3.0, 15.0, ((0, 256),)),
        "rollout_lengths": draw_rollout_lengths(jax.random.fold_in(seeds[8], 71), 0),
        "send_counts": draw_send_counts(jax.random.fold_in(seeds[8], 71), 0),
        "key_value_weight": gaussian(seeds[6], (MODEL_WIDTH, 2 * KEY_VALUE_HEADS * HEAD_SIZE), MODEL_WIDTH ** -0.5, 0.125, ((0, 16),)),
        "head_slice": gaussian(seeds[7], (MODEL_WIDTH, VOCAB_SLICE), (MODEL_WIDTH // 9) ** -0.5, 0.375, ((0, 16),)),
    }


EPS = 1e-06

def attend(query, key_rows, value_rows, visible):
    scores = jnp.einsum('qkgd,tkd->kgqt', query.astype(jnp.float32), key_rows.astype(jnp.float32)) * HEAD_SIZE ** (-0.5)
    scores = jnp.where(visible[None, None], scores, -1e+30)
    peak = lax.optimization_barrier(jnp.max(scores, -1, keepdims=True))
    weights = jnp.exp(scores - peak)
    probs = weights / lax.optimization_barrier(jnp.sum(weights, -1, keepdims=True))
    probs_b = probs.astype(jnp.bfloat16)
    out = jnp.einsum('kgqt,tkd->qkgd', probs_b.astype(jnp.float32), value_rows.astype(jnp.float32))
    return (probs, probs_b, out)

def attend_back(query, value_rows, probs, probs_b, out, output_gradient):
    packed_row_list = query.shape[0]
    grad_float = output_gradient.astype(jnp.float32)
    value_gradient = jnp.einsum('kgqt,qkgd->tkd', probs_b.astype(jnp.float32), grad_float)
    grad_probs = jnp.einsum('qkgd,tkd->kgqt', grad_float, value_rows.astype(jnp.float32))
    carry = jnp.einsum('qkgd,qkgd->kgq', grad_float, out)
    grad_scores = (probs * (grad_probs - carry[..., None]) * HEAD_SIZE ** (-0.5)).astype(jnp.bfloat16)
    key_gradient = jnp.einsum('kgqt,qkgd->tkd', grad_scores.astype(jnp.float32), query.astype(jnp.float32))
    joined_rows = jnp.concatenate([key_gradient.reshape(packed_row_list, KEY_VALUE_HEADS * HEAD_SIZE), value_gradient.reshape(packed_row_list, KEY_VALUE_HEADS * HEAD_SIZE)], 1)
    return joined_rows.astype(jnp.bfloat16)

def device_pass(tokens, first_layer, second_layer, teacher, lengths, key_value_weight, head_slice):
    packed_row_list = tokens.shape[0]
    ends = jnp.cumsum(lengths).astype(jnp.int32)
    position = jnp.arange(packed_row_list, dtype=jnp.int32)
    segment = lax.optimization_barrier(jnp.sum((position[:, None] >= ends[None, :]).astype(jnp.int32), 1))
    visible = (segment[:, None] == segment[None, :]) & (position[None, :] <= position[:, None])
    key_value_rows = jnp.dot(tokens, key_value_weight, preferred_element_type=jnp.float32).astype(jnp.bfloat16)
    key_rows = key_value_rows[:, :KEY_VALUE_HEADS * HEAD_SIZE].reshape(packed_row_list, KEY_VALUE_HEADS, HEAD_SIZE)
    value_rows = key_value_rows[:, KEY_VALUE_HEADS * HEAD_SIZE:].reshape(packed_row_list, KEY_VALUE_HEADS, HEAD_SIZE)
    query_upper = first_layer.reshape(packed_row_list, KEY_VALUE_HEADS, HEADS_PER_KEY, HEAD_SIZE)
    query_lower = second_layer.reshape(packed_row_list, KEY_VALUE_HEADS, HEADS_PER_KEY, HEAD_SIZE)
    probs_a, probs_ab, out_a = attend(query_upper, key_rows, value_rows, visible)
    probs_b, probs_bb, out_b = attend(query_lower, key_rows, value_rows, visible)
    hidden = tokens.astype(jnp.float32) + out_a.reshape(packed_row_list, MODEL_WIDTH) + out_b.reshape(packed_row_list, MODEL_WIDTH)
    inverse = lax.rsqrt(lax.optimization_barrier(jnp.mean(hidden * hidden, -1, keepdims=True)) + EPS)
    normed = hidden * inverse
    normed_b = normed.astype(jnp.bfloat16)
    logits = jnp.dot(normed_b, head_slice, preferred_element_type=jnp.float32)
    student = jax.nn.log_softmax(logits, -1)
    target = jax.nn.log_softmax(teacher.astype(jnp.float32), -1)
    grad_logits = (jnp.exp(student) - jnp.exp(target)).astype(jnp.bfloat16)
    head_term = jnp.dot(normed_b.T, grad_logits, preferred_element_type=jnp.float32)
    grad_normed = jnp.dot(grad_logits, head_slice.T, preferred_element_type=jnp.float32)
    hidden_gradient = inverse * (grad_normed - normed * lax.optimization_barrier(jnp.mean(grad_normed * normed, -1, keepdims=True)))
    output_gradient = hidden_gradient.astype(jnp.bfloat16).reshape(packed_row_list, KEY_VALUE_HEADS, HEADS_PER_KEY, HEAD_SIZE)
    kv_a = attend_back(query_upper, value_rows, probs_a, probs_ab, out_a, output_gradient)
    kv_b = attend_back(query_lower, value_rows, probs_b, probs_bb, out_b, output_gradient)
    kv_term = jnp.dot(tokens.T, kv_a, preferred_element_type=jnp.float32) + jnp.dot(tokens.T, kv_b, preferred_element_type=jnp.float32)
    back_a = jnp.dot(kv_a, key_value_weight.T, preferred_element_type=jnp.float32)
    back_b = jnp.dot(kv_b, key_value_weight.T, preferred_element_type=jnp.float32)
    grad_rows = (hidden_gradient + back_a + back_b).astype(jnp.bfloat16)
    return (grad_rows, kv_term, head_term)

def reference(tokens_in, queries_first, queries_second, teacher_logits, rollout_lengths, send_counts, key_value_weight, head_slice):
    devices = N_DP * N_FSDP
    blocks = (tokens_in.reshape(devices, TOK_DEV, MODEL_WIDTH), queries_first.reshape(devices, TOK_DEV, MODEL_WIDTH), queries_second.reshape(devices, TOK_DEV, MODEL_WIDTH), teacher_logits.reshape(devices, TOK_DEV, VOCAB_SLICE), rollout_lengths.reshape(devices, NR))

    def step(totals, item):
        grad_rows, kv_term, head_term = device_pass(item[0], item[1], item[2], item[3], item[4], key_value_weight, head_slice)
        return ((totals[0] + kv_term, totals[1] + head_term), grad_rows)
    starting_sums = (jnp.zeros((MODEL_WIDTH, 2 * KEY_VALUE_HEADS * HEAD_SIZE), jnp.float32), jnp.zeros((MODEL_WIDTH, VOCAB_SLICE), jnp.float32))
    (kv_grad, head_grad), moved = lax.scan(step, starting_sums, blocks)
    zero = jnp.zeros((N_DP, N_FSDP, 1), jnp.int32)
    len_cum = jnp.concatenate([zero, jnp.cumsum(rollout_lengths, -1).astype(jnp.int32)], -1)
    count_end = jnp.cumsum(send_counts, -1).astype(jnp.int32)
    count_start = count_end - send_counts
    row_start = jnp.take_along_axis(len_cum, count_start, -1)
    row_end = jnp.take_along_axis(len_cum, count_end, -1)
    sizes = row_end - row_start
    offsets = jnp.cumsum(sizes, 0).astype(jnp.int32) - sizes
    position = jnp.arange(TOK_DEV, dtype=jnp.int32)
    dest = lax.optimization_barrier(jnp.sum((position[None, None, :, None] >= row_end[:, :, None, :]).astype(jnp.int32), -1))
    within = position[None, None, :] - jnp.take_along_axis(row_start, dest, -1)
    place = jnp.take_along_axis(offsets, dest, -1) + within
    fsdp_index = jnp.arange(N_FSDP, dtype=jnp.int32)[None, :, None]
    target_rows = ((dest * N_FSDP + fsdp_index) * TOK_DEV + place).astype(jnp.int32)
    input_grad = jnp.zeros((TOKENS, MODEL_WIDTH), jnp.bfloat16).at[target_rows.reshape(-1)].set(moved.reshape(-1, MODEL_WIDTH))
    return (input_grad, kv_grad, head_grad)
```

```python
import jax
import jax.numpy as jnp
from jax import lax
from jax.sharding import PartitionSpec as P

KEY_VALUE_HEADS = 4
HEADS_PER_KEY = 5
HEAD_SIZE = 128


EPS = 1e-06


def pick(table, index):
    slots = jnp.arange(table.shape[-1], dtype=jnp.int32)
    match = (index[..., :, None] == slots).astype(jnp.int32)
    return jnp.sum(table[..., None, :] * match, -1)


def piece_bounds(lengths, counts):
    zero = jnp.zeros(lengths.shape[:-1] + (1,), jnp.int32)
    len_cum = jnp.concatenate([zero, jnp.cumsum(lengths, -1)], -1)
    count_end = jnp.cumsum(counts, -1)
    begin = pick(len_cum, count_end - counts)
    return (len_cum, begin, pick(len_cum, count_end) - begin)


def pack_rows(source_array, begin, size, width):
    slot = jnp.arange(width, dtype=jnp.int32)
    index = begin[:, None] + slot[None, :]
    keep = slot[None, :] < size[:, None]
    flat = jnp.minimum(index, source_array.shape[0] - 1).reshape(-1)
    taken = source_array[flat].reshape(index.shape + (source_array.shape[1],))
    return jnp.where(keep[..., None], taken, jnp.zeros((), source_array.dtype))


def arrival(size_in, packed_row_list, width):
    offset_end = jnp.cumsum(size_in)
    offset = offset_end - size_in
    position = jnp.arange(packed_row_list, dtype=jnp.int32)
    source = jnp.sum((position[:, None] >= offset_end[None, :]).astype(jnp.int32), 1)
    within = position - pick(offset[None, :], source[None, :])[0]
    return (source, within, source * width + within)


def unpack_rows(received, index):
    return received.reshape(-1, received.shape[-1])[index]


def attend(query, key_rows, value_rows, visible):
    scores = jnp.einsum(
        "qkgd,tkd->kgqt", query, key_rows, preferred_element_type=jnp.float32
    ) * HEAD_SIZE ** (-0.5)
    scores = jnp.where(visible, scores, -1e30)
    peak = jnp.max(scores, -1, keepdims=True)
    weights = jnp.exp(scores - peak)
    probs = weights / jnp.sum(weights, -1, keepdims=True)
    probs_b = probs.astype(jnp.bfloat16)
    out = jnp.einsum("kgqt,tkd->qkgd", probs_b, value_rows, preferred_element_type=jnp.float32)
    return (probs, probs_b, out)


def attend_back(query, value_rows, probs, probs_b, out, output_gradient):
    packed_row_list = query.shape[0]
    value_gradient = jnp.einsum(
        "kgqt,qkgd->tkd", probs_b, output_gradient, preferred_element_type=jnp.float32
    )
    grad_probs = jnp.einsum(
        "qkgd,tkd->kgqt", output_gradient, value_rows, preferred_element_type=jnp.float32
    )
    carry = jnp.einsum("qkgd,qkgd->kgq", output_gradient.astype(jnp.float32), out)
    grad_scores = (probs * (grad_probs - carry[..., None]) * HEAD_SIZE ** (-0.5)).astype(
        jnp.bfloat16
    )
    key_gradient = jnp.einsum(
        "kgqt,qkgd->tkd", grad_scores, query, preferred_element_type=jnp.float32
    )
    joined_rows = jnp.concatenate(
        [
            key_gradient.reshape(packed_row_list, KEY_VALUE_HEADS * HEAD_SIZE),
            value_gradient.reshape(packed_row_list, KEY_VALUE_HEADS * HEAD_SIZE),
        ],
        1,
    )
    return joined_rows.astype(jnp.bfloat16)


def pair_pass(tokens, first_layer, second_layer, teacher, segment, w_full, head_full):
    packed_row_list = tokens.shape[0]
    position = jnp.arange(packed_row_list, dtype=jnp.int32)
    visible = (segment[:, None] == segment[None, :]) & (position[None, :] <= position[:, None])
    key_value_rows = jnp.dot(tokens, w_full, preferred_element_type=jnp.float32).astype(
        jnp.bfloat16
    )
    key_rows = key_value_rows[:, : KEY_VALUE_HEADS * HEAD_SIZE].reshape(
        packed_row_list, KEY_VALUE_HEADS, HEAD_SIZE
    )
    value_rows = key_value_rows[:, KEY_VALUE_HEADS * HEAD_SIZE :].reshape(
        packed_row_list, KEY_VALUE_HEADS, HEAD_SIZE
    )
    query_upper = first_layer.reshape(packed_row_list, KEY_VALUE_HEADS, HEADS_PER_KEY, HEAD_SIZE)
    query_lower = second_layer.reshape(packed_row_list, KEY_VALUE_HEADS, HEADS_PER_KEY, HEAD_SIZE)
    probs_a, probs_ab, out_a = attend(query_upper, key_rows, value_rows, visible)
    probs_b, probs_bb, out_b = attend(query_lower, key_rows, value_rows, visible)
    width = tokens.shape[1]
    hidden = (
        tokens.astype(jnp.float32)
        + out_a.reshape(packed_row_list, width)
        + out_b.reshape(packed_row_list, width)
    )
    inverse = lax.rsqrt(jnp.mean(hidden * hidden, -1, keepdims=True) + EPS)
    normed = hidden * inverse
    normed_b = normed.astype(jnp.bfloat16)
    logits = jnp.dot(normed_b, head_full, preferred_element_type=jnp.float32)
    student = jax.nn.log_softmax(logits, -1)
    target = jax.nn.log_softmax(teacher.astype(jnp.float32), -1)
    grad_logits = (jnp.exp(student) - jnp.exp(target)).astype(jnp.bfloat16)
    grad_normed = lax.dot_general(
        grad_logits, head_full, (((1,), (1,)), ((), ())), preferred_element_type=jnp.float32
    )
    hidden_gradient = inverse * (
        grad_normed - normed * jnp.mean(grad_normed * normed, -1, keepdims=True)
    )
    output_gradient = hidden_gradient.astype(jnp.bfloat16).reshape(
        packed_row_list, KEY_VALUE_HEADS, HEADS_PER_KEY, HEAD_SIZE
    )
    kv_a = attend_back(query_upper, value_rows, probs_a, probs_ab, out_a, output_gradient)
    kv_b = attend_back(query_lower, value_rows, probs_b, probs_bb, out_b, output_gradient)
    back_a = lax.dot_general(
        kv_a, w_full, (((1,), (1,)), ((), ())), preferred_element_type=jnp.float32
    )
    back_b = lax.dot_general(
        kv_b, w_full, (((1,), (1,)), ((), ())), preferred_element_type=jnp.float32
    )
    grad_rows = (hidden_gradient + back_a + back_b).astype(jnp.bfloat16)
    return (grad_rows, kv_a, kv_b, normed_b, grad_logits)


def on_device(
    tokens_in,
    queries_first,
    queries_second,
    teacher_logits,
    rollout_lengths,
    send_counts,
    key_value_weight,
    head_slice,
):
    groups = lax.axis_size("dp")
    here = lax.axis_index("dp")
    packed_row_list = tokens_in.shape[0]
    width = 3 * packed_row_list // (2 * groups)
    lengths = rollout_lengths[:, 0, :]
    counts = send_counts[:, 0, :]
    len_cum, begin, size = piece_bounds(lengths, counts)
    my_begin = lax.dynamic_index_in_dim(begin, here, 0, keepdims=False)
    my_size = lax.dynamic_index_in_dim(size, here, 0, keepdims=False)
    size_in = lax.dynamic_index_in_dim(size, here, 1, keepdims=False)
    w_full, head_full = (
        lax.all_gather(key_value_weight, "fsdp", axis=0, tiled=True),
        lax.all_gather(head_slice, "fsdp", axis=0, tiled=True),
    )
    own_ends = lax.dynamic_index_in_dim(len_cum, here, 0, keepdims=False)[1:]
    position = jnp.arange(packed_row_list, dtype=jnp.int32)
    segment = jnp.sum((position[:, None] >= own_ends[None, :]).astype(jnp.int32), 1)
    tokens = tokens_in
    grad_rows, kv_a, kv_b, normed_b, grad_logits = pair_pass(
        tokens, queries_first, queries_second, teacher_logits, segment, w_full, head_full
    )
    send_rows = pack_rows(grad_rows, my_begin, my_size, width)
    got_rows = lax.all_to_all(send_rows, "dp", split_axis=0, concat_axis=0, tiled=True)
    source, within, index = arrival(size_in, packed_row_list, width)
    grad_rows = unpack_rows(got_rows, index)
    part = tokens
    first_term = lax.dot_general(
        part, kv_a, (((0,), (0,)), ((), ())), preferred_element_type=jnp.float32
    )
    second_term = lax.dot_general(
        part, kv_b, (((0,), (0,)), ((), ())), preferred_element_type=jnp.float32
    )
    kv_shard = lax.psum_scatter(
        (first_term + second_term).astype(jnp.bfloat16), "fsdp", scatter_dimension=0, tiled=True
    )
    part = normed_b
    head_shard = lax.psum_scatter(
        lax.dot_general(
            part, grad_logits, (((0,), (0,)), ((), ())), preferred_element_type=jnp.float32
        ).astype(jnp.bfloat16),
        "fsdp",
        scatter_dimension=0,
        tiled=True,
    )
    kv_total, head_total = (
        lax.psum(kv_shard, "dp").astype(jnp.float32),
        lax.psum(head_shard, "dp").astype(jnp.float32),
    )
    return (grad_rows, kv_total, head_total)


def solution(mesh):
    in_specs = (
        P(("dp", "fsdp"), None),
        P(("dp", "fsdp"), None),
        P(("dp", "fsdp"), None),
        P(("dp", "fsdp"), None),
        P(None, "fsdp", None),
        P(None, "fsdp", None),
        P("fsdp", None),
        P("fsdp", None),
    )
    out_specs = (P(("dp", "fsdp"), None), P("fsdp", None), P("fsdp", None))
    return jax.shard_map(
        on_device, mesh=mesh, in_specs=in_specs, out_specs=out_specs, check_vma=False
    )
```

```python
import functools

import jax
import jax.numpy as jnp
from jax import lax
from jax.experimental import pallas as pl
from jax.experimental.pallas import tpu as pltpu
from jax.sharding import PartitionSpec as P

ROWS = 128
WIDTH = 2560
HEADS = 20
KV_HEADS = 4
PER_KEY = 5
D = 128
KV = 1024
VOCAB = 256
SHARD = 160
HALF = 80
Z = 8
EPS = 1e-06
SCALE = D ** (-0.5)
LOG2E = 1.4426950408889634
MESH = pl.DeviceIdType.MESH
F32 = jnp.float32
BF16 = jnp.bfloat16
COPIES = 160


def iota(shape, dim):
    return lax.broadcasted_iota(jnp.int32, shape, dim)


def dot(a, b):
    return jnp.dot(a, b, preferred_element_type=F32)


def dot_nt(a, b):
    return lax.dot_general(a, b, (((1,), (1,)), ((), ())), preferred_element_type=F32)


def lanes(block, size=D):
    return pl.ds(pl.multiple_of(block * D, D), size)


def rows_at(start, size, unit=16):
    return pl.ds(pl.multiple_of(start, unit), size)


class Wires:
    def __init__(self, send, recv, here):
        self.send, self.recv, self.here = send, recv, here
        self.count = 0
        self.open = []

    def start(self, src, dst, to):
        n = self.count
        self.count += 1
        copy = pltpu.make_async_remote_copy(
            src_ref=src, dst_ref=dst, send_sem=self.send.at[n], recv_sem=self.recv.at[n],
            device_id=to, device_id_type=MESH,
        )
        copy.start()
        self.open.append(copy)
        return n

    def arrived(self, n, landed):
        pltpu.make_async_remote_copy(
            src_ref=landed, dst_ref=landed, send_sem=self.send.at[n], recv_sem=self.recv.at[n],
            device_id=self.here, device_id_type=MESH,
        ).wait_recv()

    def drain(self):
        for copy in self.open:
            copy.wait_send()


def kernel(
    tok_h, q1_h, q2_h, tea_h, len_ref, cnt_ref, w_h, head_h,
    rows_out, kv_out, head_out,
    tok, q1, q2, tea, w_full, head_full, kv, probs, probs_b, hidden, grad_h, grad_o, normed_b,
    tok_t, norm_t, tok_t_all, norm_t_all, kvg_all, gl_all, grad_rows, pack, unpack,
    part, y_in, z_out, z_in, kv_sum, hpart, hy_in, hz_in, head_sum,
    send_sem, recv_sem, local_sem,
):
    g, f = lax.axis_index("dp"), lax.axis_index("fsdp")
    z, lo = g // 2, g % 2
    hi, x, c = f // 8, (f // 2) % 4, f % 2

    def at(z_, lo_, hi_, x_, c_):
        return (z_ * 2 + lo_, hi_ * 8 + x_ * 2 + c_)

    def xk(k):
        return (x + k) % 4

    def zk(k):
        return (z + k) % Z

    other = at(z, lo, hi, x, 1 - c)
    y_far = at(z, 1 - lo, 1 - hi, x, c)
    y_pair = at(z, 1 - lo, hi, x, c)
    y_two = at(z, lo, 1 - hi, x, c)

    loads = []
    for n, (src, dst) in enumerate(((tok_h, tok), (q1_h, q1), (q2_h, q2), (tea_h, tea))):
        load = pltpu.make_async_copy(src, dst, local_sem.at[n])
        load.start()
        loads.append(load)
    own_rows = rows_at(f * SHARD, SHARD)
    for n, (src, dst) in enumerate(((w_h, w_full), (head_h, head_full))):
        load = pltpu.make_async_copy(src, dst.at[own_rows], local_sem.at[4 + n])
        load.start()
        loads.append(load)

    peers = [other, y_far, y_two]
    for k in (1, 2, 3):
        peers += [at(z, lo, hi, xk(k), c), at(z, lo, hi, xk(k), 1 - c)]
    for k in range(16):
        if k:
            peers.append(((g + k) % 16, f))
    barrier = pltpu.get_barrier_semaphore()
    for peer in peers:
        pl.semaphore_signal(barrier, inc=1, device_id=peer, device_id_type=MESH)
    pl.semaphore_wait(barrier, len(peers))

    wires = Wires(send_sem, recv_sem, other)

    def shard(full, hi_, x_, c_):
        return full.at[rows_at((hi_ * 8 + x_ * 2 + c_) * SHARD, SHARD)]

    def half(full, hi_, x_, c_, lo_):
        return full.at[rows_at((hi_ * 8 + x_ * 2 + c_) * SHARD + lo_ * HALF, HALF)]

    order = (0, 1, 3, 2)

    def gather_x(source, full):
        own = full.at[own_rows]
        n_x = {k: wires.start(source, own, at(z, lo, hi, xk(k), c)) for k in (1, 3, 2)}
        return n_x

    def gather_far(own_loaded, full, n_x):
        n_far, n_core = {}, []
        own_loaded.wait()
        for k in order:
            if k:
                wires.arrived(n_x[k], shard(full, hi, xk(4 - k), c))
            src = half(full, hi, xk(4 - k), c, 1 - lo)
            n_far[k] = wires.start(src, src, y_far)
            src = shard(full, hi, xk(4 - k), c)
            n_core.append((wires.start(src, src, other), shard(full, hi, xk(4 - k), 1 - c)))
        return n_far, n_core

    def gather_pair(full, n_far, n_core):
        n_pair = {}
        for k in order:
            src = half(full, 1 - hi, xk(4 - k), c, lo)
            wires.arrived(n_far[k], src)
            n_pair[k] = wires.start(src, src, y_pair)
            n_core.append((wires.start(src, src, other), half(full, 1 - hi, xk(4 - k), 1 - c, lo)))
        return n_pair

    def gather_core(full, n_pair, n_core):
        for k in order:
            src = half(full, 1 - hi, xk(4 - k), c, 1 - lo)
            wires.arrived(n_pair[k], src)
            n_core.append((wires.start(src, src, other), half(full, 1 - hi, xk(4 - k), 1 - c, 1 - lo)))
        for n, landed in n_core:
            wires.arrived(n, landed)

    n_x = gather_x(w_h, w_full)
    loads[0].wait()

    def transpose_tokens(b, carry):
        tok_t[rows_at(b * D, D, D), :] = tok[:, lanes(b)].T
        return carry

    lax.fori_loop(0, HEADS, transpose_tokens, 0)

    n_far, n_core = gather_far(loads[4], w_full, n_x)

    lens = len_ref[:, 0, :].astype(F32)
    counts = cnt_ref[:, 0, :].astype(F32)
    len_row = len_ref[g].astype(F32)
    cnt_row = cnt_ref[g].astype(F32)

    def lane_sum(a):
        return jnp.sum(a, axis=1, keepdims=True)

    def row_sum(a):
        return jnp.sum(a, axis=0, keepdims=True)

    ends_col = lane_sum(jnp.where(iota((32, 32), 1) <= iota((32, 32), 0), len_row, 0.0))
    len_col = lane_sum(jnp.where(iota((32, 32), 1) == iota((32, 32), 0), len_row, 0.0))
    ends_row = row_sum(jnp.where(iota((32, 32), 0) <= iota((32, 32), 1), len_col, 0.0))
    seg_col = lane_sum(jnp.where(iota((ROWS, 32), 0).astype(F32) >= ends_row, 1.0, 0.0))
    seg_row = row_sum(jnp.where(iota((32, ROWS), 1).astype(F32) >= ends_col, 1.0, 0.0))
    visible = (seg_col == seg_row) & (iota((ROWS, ROWS), 0) <= iota((ROWS, ROWS), 1))
    bias = jnp.where(visible, 0.0, -1e30).astype(F32)

    start_col = lane_sum(jnp.where(iota((16, 16), 1) < iota((16, 16), 0), cnt_row, 0.0))
    stop_col = lane_sum(jnp.where(iota((16, 16), 1) <= iota((16, 16), 0), cnt_row, 0.0))
    k_row = iota((16, 32), 1).astype(F32)
    begin_col = lane_sum(jnp.where(k_row < start_col, len_row, 0.0))
    size_col = lane_sum(jnp.where(k_row < stop_col, len_row, 0.0)) - begin_col
    spread = jnp.where(iota((256, 16), 0) // 16 == iota((256, 16), 1), 1.0, 0.0)
    begin = lane_sum(jnp.where(spread > 0.0, row_sum(jnp.where(iota((16, 16), 0) == iota((16, 16), 1), begin_col, 0.0)), 0.0))
    size = lane_sum(jnp.where(spread > 0.0, row_sum(jnp.where(iota((16, 16), 0) == iota((16, 16), 1), size_col, 0.0)), 0.0))
    slot = (iota((256, ROWS), 0) % 16).astype(F32)
    row_id = iota((256, ROWS), 1).astype(F32)
    main = jnp.where((slot < 12.0) & (slot < size) & (row_id == begin + slot), 1.0, 0.0)
    pack_lhs = []
    for r in range(3):
        w = slot - (12.0 - 4.0 * r)
        rest = jnp.where((slot >= 12.0) & (w < size) & (row_id == begin + w), 1.0, 0.0)
        pack_lhs.append(jnp.concatenate([main, rest], axis=1).astype(BF16))

    start_in = lane_sum(jnp.where(iota((16, 16), 1) < g, counts, 0.0))
    stop_in = lane_sum(jnp.where(iota((16, 16), 1) <= g, counts, 0.0))
    size_in = lane_sum(jnp.where((k_row >= start_in) & (k_row < stop_in), lens, 0.0))
    group = iota((16, 256), 1) // 16
    size_row = row_sum(jnp.where(group == iota((16, 256), 0), size_in, 0.0))
    base_row = row_sum(jnp.where(iota((16, 256), 0) < group, size_in, 0.0))
    slot = (iota((ROWS, 256), 1) % 16).astype(F32)
    place = iota((ROWS, 256), 0).astype(F32)
    unpack_main = jnp.where((slot < 12.0) & (slot < size_row) & (place == base_row + slot), 1.0, 0.0).astype(BF16)
    unpack_rest = []
    for r in range(3):
        w = slot - (12.0 - 4.0 * r)
        unpack_rest.append(jnp.where((slot >= 12.0) & (w < size_row) & (place == base_row + w), 1.0, 0.0).astype(BF16))

    n_pair = gather_pair(w_full, n_far, n_core)
    n_hx = gather_x(head_h, head_full)
    gather_core(w_full, n_pair, n_core)

    def project(b, carry):
        cols = pl.ds(pl.multiple_of(b * 256, 256), 256)
        kv[:, cols] = dot(tok[...], w_full[:, cols]).astype(BF16)
        return carry

    lax.fori_loop(0, KV // 256, project, 0)

    p = x * 2 + c

    def exchange_t(mine, everyone):
        numbers = []
        for k in (0, 1, 3, 2):
            for flip in (0, 1):
                if k == 0 and flip == 0:
                    continue
                c_to = c if flip == 0 else 1 - c
                p_to = xk(k) * 2 + c_to
                p_from = xk(4 - k) * 2 + c_to
                for h_ in (0, 1):
                    src = mine.at[rows_at(h_ * 1280 + p_to * SHARD, SHARD), :]
                    dst = everyone.at[rows_at(h_ * SHARD, SHARD), lanes(p)]
                    n = wires.start(src, dst, at(z, lo, hi, xk(k), c_to))
                    numbers.append((n, everyone.at[rows_at(h_ * SHARD, SHARD), lanes(p_from)]))
        for h_ in (0, 1):
            everyone[rows_at(h_ * SHARD, SHARD), lanes(p)] = mine[rows_at(h_ * 1280 + p * SHARD, SHARD), :]
        return numbers

    n_tok = exchange_t(tok_t, tok_t_all)
    n_hfar, n_hcore = gather_far(loads[5], head_full, n_hx)
    loads[1].wait()
    loads[2].wait()

    def softmax_cols(scores):
        s = scores * (SCALE * LOG2E) + bias
        e = jnp.exp2(s - jnp.max(s, axis=0, keepdims=True))
        return e * (1.0 / jnp.sum(e, axis=0, keepdims=True))

    def attend(j, squares):
        keys = kv[:, lanes(j)]
        values = kv[:, lanes(KV_HEADS + j)]
        for i in range(PER_KEY):
            h = j * PER_KEY + i
            one = softmax_cols(dot_nt(keys, q1[:, lanes(h)]))
            two = softmax_cols(dot_nt(keys, q2[:, lanes(h)]))
            probs[2 * h] = one
            probs[2 * h + 1] = two
            both = (one + two).astype(BF16)
            probs_b[h] = both
            hid = tok[:, lanes(h)].astype(F32) + dot(both.T, values)
            hidden[:, lanes(h)] = hid
            squares = squares + hid * hid
        return squares

    squares = lax.fori_loop(0, 2, attend, jnp.zeros((ROWS, D), F32))
    n_hpair = gather_pair(head_full, n_hfar, n_hcore)
    squares = lax.fori_loop(2, 4, attend, squares)
    inverse = lax.rsqrt(jnp.sum(squares, axis=1, keepdims=True) * (1.0 / WIDTH) + EPS)

    def normalise(b, carry):
        n_b = (hidden[:, lanes(b)] * inverse).astype(BF16)
        normed_b[:, lanes(b)] = n_b
        norm_t[rows_at(b * D, D, D), :] = n_b.T
        return carry

    lax.fori_loop(0, HEADS, normalise, 0)
    gather_core(head_full, n_hpair, n_hcore)
    loads[3].wait()

    def softmax_rows(a):
        e = jnp.exp(a - jnp.max(a, axis=1, keepdims=True))
        return e / jnp.sum(e, axis=1, keepdims=True)

    student = softmax_rows(dot(normed_b[...], head_full[...]))
    grad_logits = (student - softmax_rows(tea[...].astype(F32))).astype(BF16)
    mine = rows_at(p * ROWS, ROWS, ROWS)
    gl_all[mine, :] = grad_logits

    def ring_x(everyone, cols):
        src = everyone.at[mine, cols]
        out = {k: wires.start(src, src, at(z, lo, hi, xk(k), c)) for k in (1, 3, 2)}
        return out, [(wires.start(src, src, other), everyone.at[rows_at((x * 2 + 1 - c) * ROWS, ROWS, ROWS), cols])]

    def relay_x(everyone, cols, out, core):
        for k in (1, 3, 2):
            src = everyone.at[rows_at((xk(4 - k) * 2 + c) * ROWS, ROWS, ROWS), cols]
            wires.arrived(out[k], src)
            core.append((wires.start(src, src, other), everyone.at[rows_at((xk(4 - k) * 2 + 1 - c) * ROWS, ROWS, ROWS), cols]))

    def wait_core(core):
        for n, landed in core:
            wires.arrived(n, landed)

    gl_cols = pl.ds(0, VOCAB)
    n_gl, n_gl_core = ring_x(gl_all, gl_cols)
    n_norm = exchange_t(norm_t, norm_t_all)

    def back_head(b, dots):
        cols = pl.ds(pl.multiple_of(b * 512, 512), 512)
        gn = dot_nt(grad_logits, head_full[cols, :])
        grad_h[:, cols] = gn
        prod = gn * (hidden[:, cols] * inverse)
        for q in range(4):
            dots = dots + prod[:, q * D:(q + 1) * D]
        return dots

    dots = lax.fori_loop(0, WIDTH // 512, back_head, jnp.zeros((ROWS, D), F32))
    mean = jnp.sum(dots, axis=1, keepdims=True) * (1.0 / WIDTH)

    def back_norm(b, carry):
        cols = pl.ds(pl.multiple_of(b * 512, 512), 512)
        gh = inverse * (grad_h[:, cols] - (hidden[:, cols] * inverse) * mean)
        grad_h[:, cols] = gh
        grad_o[:, cols] = gh.astype(BF16)
        return carry

    lax.fori_loop(0, WIDTH // 512, back_norm, 0)

    def attend_back(j, carry):
        values = kv[:, lanes(KV_HEADS + j)]
        gk = jnp.zeros((ROWS, D), F32)
        gv = jnp.zeros((ROWS, D), F32)
        for i in range(PER_KEY):
            h = j * PER_KEY + i
            go = grad_o[:, lanes(h)]
            gp = dot_nt(values, go)
            gv = gv + dot(probs_b[h], go)
            for layer, queries in enumerate((q1, q2)):
                pr = probs[2 * h + layer]
                along = jnp.sum(pr * gp, axis=0, keepdims=True)
                gs = (pr * (gp - along) * SCALE).astype(BF16)
                gk = gk + dot(gs, queries[:, lanes(h)])
        kvg_all[mine, lanes(j)] = gk.astype(BF16)
        kvg_all[mine, lanes(KV_HEADS + j)] = gv.astype(BF16)
        return carry

    lax.fori_loop(0, 2, attend_back, 0)
    relay_x(gl_all, gl_cols, n_gl, n_gl_core)
    lax.fori_loop(2, 4, attend_back, 0)

    kvg_cols = pl.ds(0, KV)
    n_kvg, n_kvg_core = ring_x(kvg_all, kvg_cols)

    def back_rows(b, carry):
        cols = pl.ds(pl.multiple_of(b * 512, 512), 512)
        back = dot_nt(kvg_all[mine, :], w_full[cols, :])
        grad_rows[:, cols] = (grad_h[:, cols] + back).astype(BF16)
        return carry

    lax.fori_loop(0, WIDTH // 512, back_rows, 0)
    for e in range(5):
        rest = grad_rows[:, (15 + e) * D:(16 + e) * D]
        for r in range(3):
            b = 3 * e + r
            both = jnp.concatenate([grad_rows[:, b * D:(b + 1) * D], rest], axis=0)
            pack[:, b * D:(b + 1) * D] = dot(pack_lhs[r], both).astype(BF16)
    n_rows = []
    for k in range(1, 16):
        n = wires.start(pack.at[rows_at((g + k) % 16 * 16, 16)], unpack.at[rows_at(g * 16, 16)], ((g + k) % 16, f))
        n_rows.append((n, unpack.at[rows_at((g + 16 - k) % 16 * 16, 16)]))
    unpack[rows_at(g * 16, 16), :] = pack[rows_at(g * 16, 16), :]

    def quarter(ref, hi_, lo_):
        return ref.at[rows_at(hi_ * SHARD + lo_ * HALF, HALF), :]

    def scatter_y(ref, landing):
        out = []
        for n, (to, hi_, lo_) in enumerate(((y_far, 1 - hi, 1 - lo), (y_pair, hi, 1 - lo), (y_two, 1 - hi, lo))):
            out.append((wires.start(quarter(ref, hi_, lo_), landing.at[n], to), landing.at[n]))
        return out

    own_quarter = rows_at(hi * SHARD + lo * HALF, HALF)
    for n, landed in n_norm:
        wires.arrived(n, landed)
    wait_core(n_gl_core)
    hpart[...] = dot(norm_t_all[...], gl_all[...]).astype(BF16)
    n_hy = scatter_y(hpart, hy_in)

    relay_x(kvg_all, kvg_cols, n_kvg, n_kvg_core)
    for n, landed in n_tok:
        wires.arrived(n, landed)
    wait_core(n_kvg_core)

    def product(b, carry):
        cols = pl.ds(pl.multiple_of(b * 256, 256), 256)
        part[:, cols] = dot(tok_t_all[...], kvg_all[:, cols]).astype(BF16)
        return carry

    lax.fori_loop(0, KV // 256, product, 0)
    n_y = scatter_y(part, y_in)

    for n, landed in n_hy:
        wires.arrived(n, landed)
    total = hpart[own_quarter, :].astype(F32)
    for n in range(3):
        total = total + hy_in[n].astype(F32)
    hz_in[z] = total.astype(BF16)
    n_hz = []
    for k in (1, 7, 2, 6, 3, 5, 4):
        n = wires.start(hz_in.at[z], hz_in.at[z], at(zk(k), lo, hi, x, c))
        n_hz.append((n, hz_in.at[zk(Z - k)]))

    for n, landed in n_y:
        wires.arrived(n, landed)

    def add_y(b, carry):
        total = part[own_quarter, lanes(b)].astype(F32)
        for n in range(3):
            total = total + y_in[n, :, lanes(b)].astype(F32)
        z_out[b] = total.astype(BF16)
        return carry

    lax.fori_loop(0, Z, add_y, 0)
    n_z = []
    for k in (4, 3, 5, 2, 6, 1, 7):
        n = wires.start(z_out.at[zk(k)], z_in.at[z], at(zk(k), lo, hi, x, c))
        n_z.append((n, z_in.at[zk(Z - k)]))
    z_in[z] = z_out[z]

    for n, landed in n_hz:
        wires.arrived(n, landed)
    total = hz_in[0].astype(F32)
    for n in range(1, Z):
        total = total + hz_in[n].astype(F32)
    head_sum[lo] = total.astype(BF16)
    n_hp = wires.start(head_sum.at[lo], head_sum.at[lo], y_pair)

    for n, landed in n_z:
        wires.arrived(n, landed)
    total = z_in[0].astype(F32)
    for n in range(1, Z):
        total = total + z_in[n].astype(F32)
    kv_sum[lo, z] = total.astype(BF16)
    n_zg, n_pair = {}, []
    for k in (4, 3, 5, 2, 6, 1, 7):
        n_zg[k] = wires.start(kv_sum.at[lo, z], kv_sum.at[lo, z], at(zk(k), lo, hi, x, c))
    n_pair.append((wires.start(kv_sum.at[lo, z], kv_sum.at[lo, z], y_pair), kv_sum.at[1 - lo, z]))

    for n, landed in n_rows:
        wires.arrived(n, landed)
    rows_out[:, :15 * D] = dot(unpack_main, unpack[...]).astype(BF16)
    for e in range(5):
        acc = dot(unpack_rest[0], unpack[:, 3 * e * D:(3 * e + 1) * D])
        for r in (1, 2):
            acc = acc + dot(unpack_rest[r], unpack[:, (3 * e + r) * D:(3 * e + r + 1) * D])
        rows_out[:, (15 + e) * D:(16 + e) * D] = acc.astype(BF16)

    for k in (1, 7, 2, 6, 3, 5, 4):
        src = kv_sum.at[lo, zk(Z - k)]
        wires.arrived(n_zg[k], src)
        n_pair.append((wires.start(src, src, y_pair), kv_sum.at[1 - lo, zk(Z - k)]))
    wires.arrived(n_hp, head_sum.at[1 - lo])
    for l in range(2):
        head_out[l * HALF:(l + 1) * HALF, :] = head_sum[l].astype(F32)
    for n, landed in n_pair:
        wires.arrived(n, landed)
    for l in range(2):
        for b in range(Z):
            kv_out[l * HALF:(l + 1) * HALF, b * D:(b + 1) * D] = kv_sum[l, b].astype(F32)
    wires.drain()


def on_device(tokens_in, queries_first, queries_second, teacher_logits, rollout_lengths, send_counts, key_value_weight, head_slice):
    big = pl.BlockSpec(memory_space=pl.ANY)
    small = pl.BlockSpec(memory_space=pltpu.VMEM)

    def buf(*shape, dtype=BF16):
        return pltpu.VMEM(shape, dtype)

    return pl.pallas_call(
        kernel,
        out_shape=(
            jax.ShapeDtypeStruct((ROWS, WIDTH), BF16),
            jax.ShapeDtypeStruct((SHARD, KV), F32),
            jax.ShapeDtypeStruct((SHARD, VOCAB), F32),
        ),
        in_specs=[big, big, big, big, small, small, big, big],
        out_specs=(small, small, small),
        scratch_shapes=[
            buf(ROWS, WIDTH), buf(ROWS, WIDTH), buf(ROWS, WIDTH), buf(ROWS, VOCAB),
            buf(WIDTH, KV), buf(WIDTH, VOCAB), buf(ROWS, KV),
            buf(2 * HEADS, ROWS, D, dtype=F32), buf(HEADS, ROWS, D),
            buf(ROWS, WIDTH, dtype=F32), buf(ROWS, WIDTH, dtype=F32), buf(ROWS, WIDTH), buf(ROWS, WIDTH),
            buf(WIDTH, ROWS), buf(WIDTH, ROWS), buf(2 * SHARD, 8 * ROWS), buf(2 * SHARD, 8 * ROWS),
            buf(8 * ROWS, KV), buf(8 * ROWS, VOCAB), buf(ROWS, WIDTH),
            buf(256, 15 * D), buf(256, 15 * D),
            buf(2 * SHARD, KV), buf(3, HALF, KV), buf(Z, HALF, D), buf(Z, HALF, D), buf(2, Z, HALF, D),
            buf(2 * SHARD, VOCAB), buf(3, HALF, VOCAB), buf(Z, HALF, VOCAB), buf(2, HALF, VOCAB),
            pltpu.SemaphoreType.DMA((COPIES,)), pltpu.SemaphoreType.DMA((COPIES,)), pltpu.SemaphoreType.DMA((6,)),
        ],
        compiler_params=pltpu.CompilerParams(collective_id=0, has_side_effects=True, vmem_limit_bytes=48 * 2**20),
        name="pair_backward",
    )(tokens_in, queries_first, queries_second, teacher_logits, rollout_lengths, send_counts, key_value_weight, head_slice)


def solution(mesh):
    in_specs = (
        P(("dp", "fsdp"), None),
        P(("dp", "fsdp"), None),
        P(("dp", "fsdp"), None),
        P(("dp", "fsdp"), None),
        P(None, "fsdp", None),
        P(None, "fsdp", None),
        P("fsdp", None),
        P("fsdp", None),
    )
    out_specs = (P(("dp", "fsdp"), None), P("fsdp", None), P("fsdp", None))
    return jax.shard_map(on_device, mesh=mesh, in_specs=in_specs, out_specs=out_specs, check_vma=False)
```

```python
import functools

import jax
import jax.numpy as jnp
from jax import lax
from jax.experimental import pallas as pl
from jax.experimental.pallas import tpu as pltpu
from jax.sharding import PartitionSpec as P

ROWS = 128
WIDTH = 2560
HEADS = 20
KV_HEADS = 4
PER_KEY = 5
D = 128
KV = 1024
VOCAB = 256
SHARD = 160
HALF = 80
Z = 8
EPS = 1e-06
SCALE = D ** (-0.5)
LOG2E = 1.4426950408889634
MESH = pl.DeviceIdType.MESH
F32 = jnp.float32
BF16 = jnp.bfloat16
COPIES = 200


def iota(shape, dim):
    return lax.broadcasted_iota(jnp.int32, shape, dim)


def dot(a, b):
    return jnp.dot(a, b, preferred_element_type=F32)


def dot_nt(a, b):
    return lax.dot_general(a, b, (((1,), (1,)), ((), ())), preferred_element_type=F32)


def lanes(block, size=D):
    return pl.ds(pl.multiple_of(block * D, D), size)


def rows_at(start, size, unit=16):
    return pl.ds(pl.multiple_of(start, unit), size)


class Wires:
    def __init__(self, send, recv, here):
        self.send, self.recv, self.here = send, recv, here
        self.count = 0
        self.open = []

    def start(self, src, dst, to):
        n = self.count
        self.count += 1
        copy = pltpu.make_async_remote_copy(
            src_ref=src, dst_ref=dst, send_sem=self.send.at[n], recv_sem=self.recv.at[n],
            device_id=to, device_id_type=MESH,
        )
        copy.start()
        self.open.append(copy)
        return n

    def arrived(self, n, landed):
        pltpu.make_async_remote_copy(
            src_ref=landed, dst_ref=landed, send_sem=self.send.at[n], recv_sem=self.recv.at[n],
            device_id=self.here, device_id_type=MESH,
        ).wait_recv()

    def drain(self):
        for copy in self.open:
            copy.wait_send()


def kernel(
    tok_h, q1_h, q2_h, tea_h, len_ref, cnt_ref, w_h, head_h,
    rows_out, kv_out, head_out,
    tok, q1, q2, tea, w_full, head_full, kv, probs, probs_b, hidden, grad_h, grad_o, normed_b,
    tok_tx, tok_ty, norm_ty, tok_x_all, tok_y_all, norm_y_all, keys_all, vals_all, grad_rows, pack, unpack,
    part_x, part_y, y_in, x_in, z_out, z_in, kv_sum,
    send_sem, recv_sem, local_sem,
):
    g, f = lax.axis_index("dp"), lax.axis_index("fsdp")
    z, lo = g // 2, g % 2
    hi, x, c = f // 8, (f // 2) % 4, f % 2

    def at(z_, lo_, hi_, x_, c_):
        return (z_ * 2 + lo_, hi_ * 8 + x_ * 2 + c_)

    def xk(k):
        return (x + k) % 4

    def zk(k):
        return (z + k) % Z

    def yk(k):
        y_ = (hi * 2 + lo + k) % 4
        return y_ // 2, y_ % 2

    other = at(z, lo, hi, x, 1 - c)
    y_far = at(z, 1 - lo, 1 - hi, x, c)
    y_pair = at(z, 1 - lo, hi, x, c)
    y_two = at(z, lo, 1 - hi, x, c)

    loads = []
    for n, (src, dst) in enumerate(((tok_h, tok), (q1_h, q1), (q2_h, q2), (tea_h, tea))):
        load = pltpu.make_async_copy(src, dst, local_sem.at[n])
        load.start()
        loads.append(load)
    own_rows = rows_at(f * SHARD, SHARD)
    for n, (src, dst) in enumerate(((w_h, w_full), (head_h, head_full))):
        load = pltpu.make_async_copy(src, dst.at[own_rows], local_sem.at[4 + n])
        load.start()
        loads.append(load)

    peers = [other, y_far, y_two, at(z, 1 - lo, 1 - hi, x, 1 - c), at(z, 1 - lo, hi, x, 1 - c), at(z, lo, 1 - hi, x, 1 - c)]
    for k in (1, 2, 3):
        peers += [at(z, lo, hi, xk(k), c), at(z, lo, hi, xk(k), 1 - c)]
    for k in range(16):
        if k:
            peers.append(((g + k) % 16, f))
    barrier = pltpu.get_barrier_semaphore()
    for peer in peers:
        pl.semaphore_signal(barrier, inc=1, device_id=peer, device_id_type=MESH)
    pl.semaphore_wait(barrier, len(peers))

    wires = Wires(send_sem, recv_sem, other)

    def shard(full, hi_, x_, c_):
        return full.at[rows_at((hi_ * 8 + x_ * 2 + c_) * SHARD, SHARD)]

    def half(full, hi_, x_, c_, lo_):
        return full.at[rows_at((hi_ * 8 + x_ * 2 + c_) * SHARD + lo_ * HALF, HALF)]

    order = (0, 1, 3, 2)

    def gather_x(source, full):
        own = full.at[own_rows]
        n_x = {k: wires.start(source, own, at(z, lo, hi, xk(k), c)) for k in (1, 3, 2)}
        return n_x

    def gather_far(own_loaded, full, n_x):
        n_far, n_core = {}, []
        own_loaded.wait()
        for k in order:
            if k:
                wires.arrived(n_x[k], shard(full, hi, xk(4 - k), c))
            src = half(full, hi, xk(4 - k), c, 1 - lo)
            n_far[k] = wires.start(src, src, y_far)
            src = shard(full, hi, xk(4 - k), c)
            n_core.append((wires.start(src, src, other), shard(full, hi, xk(4 - k), 1 - c)))
        return n_far, n_core

    def gather_pair(full, n_far, n_core):
        n_pair = {}
        for k in order:
            src = half(full, 1 - hi, xk(4 - k), c, lo)
            wires.arrived(n_far[k], src)
            n_pair[k] = wires.start(src, src, y_pair)
            n_core.append((wires.start(src, src, other), half(full, 1 - hi, xk(4 - k), 1 - c, lo)))
        return n_pair

    def gather_core(full, n_pair, n_core):
        for k in order:
            src = half(full, 1 - hi, xk(4 - k), c, 1 - lo)
            wires.arrived(n_pair[k], src)
            n_core.append((wires.start(src, src, other), half(full, 1 - hi, xk(4 - k), 1 - c, 1 - lo)))

    kept = pl.ds(pl.multiple_of(z % 2 * (KV // 2), KV // 2), KV // 2)
    given = pl.ds(pl.multiple_of((1 - z % 2) * (KV // 2), KV // 2), KV // 2)

    def block(hi_, x_, c_, cols, half_=None):
        start = (hi_ * 8 + x_ * 2 + c_) * SHARD
        if half_ is None:
            return w_full.at[rows_at(start, SHARD), cols]
        return w_full.at[rows_at(start + half_ * HALF, HALF), cols]

    w_core, w_z = [], []

    def to_core(hi_, x_, cols, half_=None):
        src = block(hi_, x_, c, cols, half_)
        w_core.append((wires.start(src, src, other), block(hi_, x_, 1 - c, cols, half_)))

    def to_z(hi_, x_, half_):
        src = block(hi_, x_, c, kept, half_)
        n = wires.start(src, src, at((z + 1 - 2 * half_ + Z) % Z, lo, hi, x, c))
        w_z.append((n, hi_, x_, half_))

    def to_far(x_):
        src = block(hi, x_, c, kept, 1 - lo)
        return wires.start(src, src, y_far)

    loads[4].wait()
    n_x, n_far, n_pair = {}, {}, {}
    n_far[0] = to_far(x)
    for k, half_ in ((1, 1 - lo), (3, 1 - lo), (1, lo), (3, lo), (2, 1 - lo), (2, lo)):
        src = block(hi, x, c, kept, half_)
        n_x.setdefault(k, []).append(wires.start(src, src, at(z, lo, hi, xk(k), c)))
    to_core(hi, x, pl.ds(0, KV))
    loads[0].wait()

    def turn_rows(ref, m):
        blocks = [ref[:, lanes(5 * m + i)].T for i in range(5)]
        return jnp.concatenate(blocks, axis=0)

    def units(turned, m):
        for i in range(8):
            yield m // 2, m % 2 * 2 + i // 4, i // 2 % 2, i % 2, turned[i * HALF:(i + 1) * HALF, :]

    def y_order(h_, x_, c_, half_):
        return rows_at(((h_ * 2 + half_) * 2 + c_) * 2 * SHARD + x_ * HALF, HALF)

    def transpose_tokens(m, carry):
        for h_, x_, c_, half_, unit in units(turn_rows(tok, m), m):
            tok_tx[rows_at((x_ * 2 + c_) * 2 * SHARD + h_ * SHARD + half_ * HALF, HALF), :] = unit
            tok_ty[y_order(h_, x_, c_, half_), :] = unit
        return carry

    lax.fori_loop(0, 4, transpose_tokens, 0)

    def got_x(k, turn):
        x_ = xk(4 - k)
        half_ = lo if turn else 1 - lo
        wires.arrived(n_x[k][turn], block(hi, x_, c, kept, half_))
        to_z(hi, x_, half_)
        if not turn:
            n_far[k] = to_far(x_)
        to_core(hi, x_, kept, half_)

    def got_far(k):
        x_ = xk(4 - k)
        src = block(1 - hi, x_, c, kept, lo)
        wires.arrived(n_far[k], src)
        n_pair[k] = wires.start(src, src, y_pair)
        to_z(1 - hi, x_, lo)
        to_core(1 - hi, x_, kept, lo)

    def got_pair(k):
        x_ = xk(4 - k)
        wires.arrived(n_pair[k], block(1 - hi, x_, c, kept, 1 - lo))
        to_z(1 - hi, x_, 1 - lo)
        to_core(1 - hi, x_, kept, 1 - lo)

    got_far(0)
    got_x(1, 0)
    got_x(3, 0)
    got_x(1, 1)
    got_x(3, 1)
    got_pair(0)
    n_hx = gather_x(head_h, head_full)
    got_far(1)
    got_far(3)
    got_x(2, 0)
    got_x(2, 1)
    got_pair(1)
    got_pair(3)
    got_far(2)

    lens = len_ref[:, 0, :].astype(F32)
    counts = cnt_ref[:, 0, :].astype(F32)
    len_row = len_ref[g].astype(F32)
    cnt_row = cnt_ref[g].astype(F32)

    def lane_sum(a):
        return jnp.sum(a, axis=1, keepdims=True)

    def row_sum(a):
        return jnp.sum(a, axis=0, keepdims=True)

    ends_col = lane_sum(jnp.where(iota((32, 32), 1) <= iota((32, 32), 0), len_row, 0.0))
    len_col = lane_sum(jnp.where(iota((32, 32), 1) == iota((32, 32), 0), len_row, 0.0))
    ends_row = row_sum(jnp.where(iota((32, 32), 0) <= iota((32, 32), 1), len_col, 0.0))
    seg_col = lane_sum(jnp.where(iota((ROWS, 32), 0).astype(F32) >= ends_row, 1.0, 0.0))
    seg_row = row_sum(jnp.where(iota((32, ROWS), 1).astype(F32) >= ends_col, 1.0, 0.0))
    visible = (seg_col == seg_row) & (iota((ROWS, ROWS), 0) <= iota((ROWS, ROWS), 1))
    bias = jnp.where(visible, 0.0, -1e30).astype(F32)

    start_col = lane_sum(jnp.where(iota((16, 16), 1) < iota((16, 16), 0), cnt_row, 0.0))
    stop_col = lane_sum(jnp.where(iota((16, 16), 1) <= iota((16, 16), 0), cnt_row, 0.0))
    k_row = iota((16, 32), 1).astype(F32)
    begin_col = lane_sum(jnp.where(k_row < start_col, len_row, 0.0))
    size_col = lane_sum(jnp.where(k_row < stop_col, len_row, 0.0)) - begin_col
    spread = jnp.where(iota((256, 16), 0) // 16 == iota((256, 16), 1), 1.0, 0.0)
    begin = lane_sum(jnp.where(spread > 0.0, row_sum(jnp.where(iota((16, 16), 0) == iota((16, 16), 1), begin_col, 0.0)), 0.0))
    size = lane_sum(jnp.where(spread > 0.0, row_sum(jnp.where(iota((16, 16), 0) == iota((16, 16), 1), size_col, 0.0)), 0.0))
    slot = (iota((256, ROWS), 0) % 16).astype(F32)
    row_id = iota((256, ROWS), 1).astype(F32)
    main = jnp.where((slot < 12.0) & (slot < size) & (row_id == begin + slot), 1.0, 0.0)
    pack_lhs = []
    for r in range(3):
        w = slot - (12.0 - 4.0 * r)
        rest = jnp.where((slot >= 12.0) & (w < size) & (row_id == begin + w), 1.0, 0.0)
        pack_lhs.append(jnp.concatenate([main, rest], axis=1).astype(BF16))

    start_in = lane_sum(jnp.where(iota((16, 16), 1) < g, counts, 0.0))
    stop_in = lane_sum(jnp.where(iota((16, 16), 1) <= g, counts, 0.0))
    size_in = lane_sum(jnp.where((k_row >= start_in) & (k_row < stop_in), lens, 0.0))
    group = iota((16, 256), 1) // 16
    size_row = row_sum(jnp.where(group == iota((16, 256), 0), size_in, 0.0))
    base_row = row_sum(jnp.where(iota((16, 256), 0) < group, size_in, 0.0))
    slot = (iota((ROWS, 256), 1) % 16).astype(F32)
    place = iota((ROWS, 256), 0).astype(F32)
    unpack_main = jnp.where((slot < 12.0) & (slot < size_row) & (place == base_row + slot), 1.0, 0.0).astype(BF16)
    unpack_rest = []
    for r in range(3):
        w = slot - (12.0 - 4.0 * r)
        unpack_rest.append(jnp.where((slot >= 12.0) & (w < size_row) & (place == base_row + w), 1.0, 0.0).astype(BF16))

    got_pair(2)
    n_hfar, n_hcore = gather_far(loads[5], head_full, n_hx)
    n_hpair = None
    for i, (n, hi_, x_, half_) in enumerate(w_z):
        if i == 10:
            n_hpair = gather_pair(head_full, n_hfar, n_hcore)
        wires.arrived(n, block(hi_, x_, c, given, half_))
        to_core(hi_, x_, given, half_)
    for n, landed in w_core:
        wires.arrived(n, landed)

    def project(b, carry):
        cols = pl.ds(pl.multiple_of(b * 256, 256), 256)
        kv[:, cols] = dot(tok[...], w_full[:, cols]).astype(BF16)
        return carry

    lax.fori_loop(0, KV // 256, project, 0)

    def on_ring(along_x, k, c_):
        if along_x:
            return at(z, lo, hi, xk(k), c_), xk(k) * 2 + c_
        hi_, lo_ = yk(k)
        return at(z, lo_, hi_, x, c_), (hi_ * 2 + lo_) * 2 + c_

    def exchange_t(mine, everyone, along_x):
        numbers = []
        spot = on_ring(along_x, 0, c)[1]
        for k, c_ in ((1, c), (3, c), (1, 1 - c), (3, 1 - c), (2, c), (2, 1 - c), (0, 1 - c)):
            to, p_to = on_ring(along_x, k, c_)
            p_from = on_ring(along_x, 4 - k, c_)[1]
            n = wires.start(mine.at[rows_at(p_to * 2 * SHARD, 2 * SHARD), :], everyone.at[:, lanes(spot)], to)
            numbers.append((n, everyone.at[:, lanes(p_from)]))
        everyone[:, lanes(spot)] = mine[rows_at(spot * 2 * SHARD, 2 * SHARD), :]
        return numbers

    n_tx = exchange_t(tok_tx, tok_x_all, True)
    n_ty = exchange_t(tok_ty, tok_y_all, False)
    loads[1].wait()
    loads[2].wait()

    def softmax_cols(scores):
        s = scores * (SCALE * LOG2E) + bias
        e = jnp.exp2(s - jnp.max(s, axis=0, keepdims=True))
        return e * (1.0 / jnp.sum(e, axis=0, keepdims=True))

    def attend(j, squares):
        keys = kv[:, lanes(j)]
        values = kv[:, lanes(KV_HEADS + j)]
        for i in range(PER_KEY):
            h = j * PER_KEY + i
            one = softmax_cols(dot_nt(keys, q1[:, lanes(h)]))
            two = softmax_cols(dot_nt(keys, q2[:, lanes(h)]))
            probs[2 * h] = one
            probs[2 * h + 1] = two
            both = (one + two).astype(BF16)
            probs_b[h] = both
            hid = tok[:, lanes(h)].astype(F32) + dot(both.T, values)
            hidden[:, lanes(h)] = hid
            squares = squares + hid * hid
        return squares

    squares = lax.fori_loop(0, 2, attend, jnp.zeros((ROWS, D), F32))
    gather_core(head_full, n_hpair, n_hcore)
    squares = lax.fori_loop(2, 4, attend, squares)
    inverse = lax.rsqrt(jnp.sum(squares, axis=1, keepdims=True) * (1.0 / WIDTH) + EPS)

    def normalise(m, carry):
        cols = pl.ds(pl.multiple_of(m * 640, 640), 640)
        normed_b[:, cols] = (hidden[:, cols] * inverse).astype(BF16)
        for h_, x_, c_, half_, unit in units(turn_rows(normed_b, m), m):
            norm_ty[y_order(h_, x_, c_, half_), :] = unit
        return carry

    lax.fori_loop(0, 4, normalise, 0)
    n_norm = exchange_t(norm_ty, norm_y_all, False)
    for n, landed in n_hcore:
        wires.arrived(n, landed)
    loads[3].wait()

    def softmax_rows(a):
        e = jnp.exp(a - jnp.max(a, axis=1, keepdims=True))
        return e / jnp.sum(e, axis=1, keepdims=True)

    student = softmax_rows(dot(normed_b[...], head_full[...]))
    grad_logits = (student - softmax_rows(tea[...].astype(F32))).astype(BF16)
    mine_x = rows_at(on_ring(True, 0, c)[1] * ROWS, ROWS, ROWS)
    mine_y = rows_at(on_ring(False, 0, c)[1] * ROWS, ROWS, ROWS)
    gl_cols = pl.ds(KV // 2, VOCAB)
    vals_all[mine_y, gl_cols] = grad_logits

    def ring_send(everyone, cols, along_x):
        src = everyone.at[rows_at(on_ring(along_x, 0, c)[1] * ROWS, ROWS, ROWS), cols]
        out = {k: wires.start(src, src, on_ring(along_x, k, c)[0]) for k in (1, 3, 2)}
        landed = everyone.at[rows_at(on_ring(along_x, 0, 1 - c)[1] * ROWS, ROWS, ROWS), cols]
        return out, [(wires.start(src, src, other), landed)]

    def ring_relay(everyone, cols, along_x, out, core):
        for k in (1, 3, 2):
            src = everyone.at[rows_at(on_ring(along_x, 4 - k, c)[1] * ROWS, ROWS, ROWS), cols]
            wires.arrived(out[k], src)
            landed = everyone.at[rows_at(on_ring(along_x, 4 - k, 1 - c)[1] * ROWS, ROWS, ROWS), cols]
            core.append((wires.start(src, src, other), landed))

    def wait_all(numbers):
        for n, landed in numbers:
            wires.arrived(n, landed)

    n_gl = ring_send(vals_all, gl_cols, False)

    def back_head(b, dots):
        cols = pl.ds(pl.multiple_of(b * 512, 512), 512)
        gn = dot_nt(grad_logits, head_full[cols, :])
        grad_h[:, cols] = gn
        prod = gn * (hidden[:, cols] * inverse)
        for q in range(4):
            dots = dots + prod[:, q * D:(q + 1) * D]
        return dots

    dots = lax.fori_loop(0, WIDTH // 512, back_head, jnp.zeros((ROWS, D), F32))
    mean = jnp.sum(dots, axis=1, keepdims=True) * (1.0 / WIDTH)

    def back_norm(b, carry):
        cols = pl.ds(pl.multiple_of(b * 512, 512), 512)
        gh = inverse * (grad_h[:, cols] - (hidden[:, cols] * inverse) * mean)
        grad_h[:, cols] = gh
        grad_o[:, cols] = gh.astype(BF16)
        return carry

    lax.fori_loop(0, WIDTH // 512, back_norm, 0)

    def attend_back(j, carry):
        values = kv[:, lanes(KV_HEADS + j)]
        gk = jnp.zeros((ROWS, D), F32)
        gv = jnp.zeros((ROWS, D), F32)
        for i in range(PER_KEY):
            h = j * PER_KEY + i
            go = grad_o[:, lanes(h)]
            gp = dot_nt(values, go)
            gv = gv + dot(probs_b[h], go)
            for layer, queries in enumerate((q1, q2)):
                pr = probs[2 * h + layer]
                along = jnp.sum(pr * gp, axis=0, keepdims=True)
                gs = (pr * (gp - along) * SCALE).astype(BF16)
                gk = gk + dot(gs, queries[:, lanes(h)])
        keys_all[mine_x, lanes(j)] = gk.astype(BF16)
        vals_all[mine_y, lanes(j)] = gv.astype(BF16)
        return carry

    lax.fori_loop(0, KV_HEADS, attend_back, 0)

    kv_cols = pl.ds(0, KV // 2)
    n_keys = ring_send(keys_all, kv_cols, True)
    n_vals = ring_send(vals_all, kv_cols, False)

    def back_rows(b, carry):
        cols = pl.ds(pl.multiple_of(b * 512, 512), 512)
        back = dot_nt(keys_all[mine_x, :], w_full[cols, :KV // 2]) + dot_nt(vals_all[mine_y, kv_cols], w_full[cols, KV // 2:])
        grad_rows[:, cols] = (grad_h[:, cols] + back).astype(BF16)
        return carry

    lax.fori_loop(0, WIDTH // 512, back_rows, 0)
    for e in range(5):
        rest = grad_rows[:, (15 + e) * D:(16 + e) * D]
        for r in range(3):
            b = 3 * e + r
            both = jnp.concatenate([grad_rows[:, b * D:(b + 1) * D], rest], axis=0)
            pack[:, b * D:(b + 1) * D] = dot(pack_lhs[r], both).astype(BF16)
    n_rows = []
    for k in (8, 7, 9, 6, 10, 5, 11, 4, 12, 3, 13, 2, 14, 1, 15):
        n = wires.start(pack.at[rows_at((g + k) % 16 * 16, 16)], unpack.at[rows_at(g * 16, 16)], ((g + k) % 16, f))
        n_rows.append((n, unpack.at[rows_at((g + 16 - k) % 16 * 16, 16)]))
    unpack[rows_at(g * 16, 16), :] = pack[rows_at(g * 16, 16), :]

    ring_relay(keys_all, kv_cols, True, *n_keys)
    ring_relay(vals_all, gl_cols, False, *n_gl)
    wait_all(n_tx)
    wait_all(n_keys[1])
    part_x[...] = dot(tok_x_all[...], keys_all[...]).astype(BF16)
    n_y = []
    for k in (1, 3, 2):
        hi_, lo_ = yk(k)
        n = wires.start(part_x.at[rows_at(hi_ * SHARD + lo_ * HALF, HALF), :], y_in.at[k - 1], on_ring(False, k, c)[0])
        n_y.append((n, y_in.at[k - 1]))

    ring_relay(vals_all, kv_cols, False, *n_vals)
    wait_all(n_ty)
    wait_all(n_norm)
    wait_all(n_gl[1])
    wait_all(n_vals[1])
    part_y[:, kv_cols] = dot(tok_y_all[...], vals_all[:, kv_cols]).astype(BF16)
    part_y[:, gl_cols] = dot(norm_y_all[...], vals_all[:, gl_cols]).astype(BF16)
    for k in (1, 3, 2):
        n = wires.start(part_y.at[rows_at(xk(k) * HALF, HALF), :], x_in.at[k - 1], on_ring(True, k, c)[0])
        n_y.append((n, x_in.at[k - 1]))
    own_x = rows_at(hi * SHARD + lo * HALF, HALF)
    own_y = rows_at(x * HALF, HALF)

    wait_all(n_y)

    def add(own, parts, cols):
        total = own.astype(F32)
        for n in range(3):
            total = total + parts[n, :, cols].astype(F32)
        return total.astype(BF16)

    def add_ring(b, carry):
        z_out[b, :HALF, :] = add(part_x[own_x, lanes(b)], y_in, lanes(b))
        z_out[b + 4, :HALF, :] = add(part_y[own_y, lanes(b)], x_in, lanes(b))
        return carry

    lax.fori_loop(0, 4, add_ring, 0)
    for v in range(2):
        cols = slice(KV // 2 + v * D, KV // 2 + (v + 1) * D)
        total = add(part_y[own_y, cols], x_in, cols)
        for b in range(Z):
            rows = total[b * 16:(b + 1) * 16] if b < 5 else jnp.zeros((16, D), BF16)
            z_out[b, HALF + v * 16:HALF + (v + 1) * 16, :] = rows
    n_z = []
    for k in (4, 3, 5, 2, 6, 1, 7):
        n = wires.start(z_out.at[zk(k)], z_in.at[z], at(zk(k), lo, hi, x, c))
        n_z.append((n, z_in.at[zk(Z - k)]))
    z_in[z] = z_out[z]

    for n, landed in n_z:
        wires.arrived(n, landed)
    total = z_in[0].astype(F32)
    for n in range(1, Z):
        total = total + z_in[n].astype(F32)
    kv_sum[lo, z] = total.astype(BF16)
    n_zg, n_pair = {}, []
    for k in (4, 3, 5, 2, 6, 1, 7):
        n_zg[k] = wires.start(kv_sum.at[lo, z], kv_sum.at[lo, z], at(zk(k), lo, hi, x, c))
    n_pair.append((wires.start(kv_sum.at[lo, z], kv_sum.at[lo, z], y_pair), kv_sum.at[1 - lo, z]))

    for n, landed in n_rows:
        wires.arrived(n, landed)
    rows_out[:, :15 * D] = dot(unpack_main, unpack[...]).astype(BF16)
    for e in range(5):
        acc = dot(unpack_rest[0], unpack[:, 3 * e * D:(3 * e + 1) * D])
        for r in (1, 2):
            acc = acc + dot(unpack_rest[r], unpack[:, (3 * e + r) * D:(3 * e + r + 1) * D])
        rows_out[:, (15 + e) * D:(16 + e) * D] = acc.astype(BF16)

    for k in (1, 7, 2, 6, 3, 5, 4):
        src = kv_sum.at[lo, zk(Z - k)]
        wires.arrived(n_zg[k], src)
        n_pair.append((wires.start(src, src, y_pair), kv_sum.at[1 - lo, zk(Z - k)]))
    for n, landed in n_pair:
        wires.arrived(n, landed)
    for l in range(2):
        for b in range(Z):
            kv_out[l * HALF:(l + 1) * HALF, b * D:(b + 1) * D] = kv_sum[l, b, :HALF, :].astype(F32)
        for b in range(5):
            for v in range(2):
                rows = kv_sum[l, b, HALF + v * 16:HALF + (v + 1) * 16, :].astype(F32)
                head_out[l * HALF + b * 16:l * HALF + (b + 1) * 16, v * D:(v + 1) * D] = rows
    wires.drain()


def on_device(tokens_in, queries_first, queries_second, teacher_logits, rollout_lengths, send_counts, key_value_weight, head_slice):
    big = pl.BlockSpec(memory_space=pltpu.HBM)
    small = pl.BlockSpec(memory_space=pltpu.VMEM)

    def buf(*shape, dtype=BF16):
        return pltpu.VMEM(shape, dtype)

    return pl.pallas_call(
        kernel,
        out_shape=(
            jax.ShapeDtypeStruct((ROWS, WIDTH), BF16),
            jax.ShapeDtypeStruct((SHARD, KV), F32),
            jax.ShapeDtypeStruct((SHARD, VOCAB), F32),
        ),
        in_specs=[big, big, big, big, small, small, big, big],
        out_specs=(small, small, small),
        scratch_shapes=[
            buf(ROWS, WIDTH), buf(ROWS, WIDTH), buf(ROWS, WIDTH), buf(ROWS, VOCAB),
            buf(WIDTH, KV), buf(WIDTH, VOCAB), buf(ROWS, KV),
            buf(2 * HEADS, ROWS, D, dtype=F32), buf(HEADS, ROWS, D),
            buf(ROWS, WIDTH, dtype=F32), buf(ROWS, WIDTH, dtype=F32), buf(ROWS, WIDTH), buf(ROWS, WIDTH),
            buf(WIDTH, ROWS), buf(WIDTH, ROWS), buf(WIDTH, ROWS),
            buf(2 * SHARD, 8 * ROWS), buf(2 * SHARD, 8 * ROWS), buf(2 * SHARD, 8 * ROWS),
            buf(8 * ROWS, KV // 2), buf(8 * ROWS, KV // 2 + VOCAB), buf(ROWS, WIDTH),
            buf(256, 15 * D), buf(256, 15 * D),
            buf(2 * SHARD, KV // 2), buf(2 * SHARD, KV // 2 + VOCAB), buf(3, HALF, KV // 2), buf(3, HALF, KV // 2 + VOCAB),
            buf(Z, HALF + 32, D), buf(Z, HALF + 32, D), buf(2, Z, HALF + 32, D),
            pltpu.SemaphoreType.DMA((COPIES,)), pltpu.SemaphoreType.DMA((COPIES,)), pltpu.SemaphoreType.DMA((6,)),
        ],
        compiler_params=pltpu.CompilerParams(collective_id=0, has_side_effects=True, vmem_limit_bytes=60 * 2**20),
        name="pair_backward",
    )(tokens_in, queries_first, queries_second, teacher_logits, rollout_lengths, send_counts, key_value_weight, head_slice)


def solution(mesh):
    in_specs = (
        P(("dp", "fsdp"), None),
        P(("dp", "fsdp"), None),
        P(("dp", "fsdp"), None),
        P(("dp", "fsdp"), None),
        P(None, "fsdp", None),
        P(None, "fsdp", None),
        P("fsdp", None),
        P("fsdp", None),
    )
    out_specs = (P(("dp", "fsdp"), None), P("fsdp", None), P("fsdp", None))
    return jax.shard_map(on_device, mesh=mesh, in_specs=in_specs, out_specs=out_specs, check_vma=False)
```

```python
import functools

import jax
import jax.numpy as jnp
from jax import lax
from jax.experimental import pallas as pl
from jax.experimental.pallas import tpu as pltpu
from jax.sharding import PartitionSpec as P

ROWS = 128
WIDTH = 2560
HEADS = 20
KV_HEADS = 4
PER_KEY = 5
D = 128
KV = 1024
VOCAB = 256
SHARD = 160
HALF = 80
Z = 8
EPS = 1e-06
SCALE = D ** (-0.5)
LOG2E = 1.4426950408889634
MESH = pl.DeviceIdType.MESH
F32 = jnp.float32
BF16 = jnp.bfloat16
COPIES = 200


def iota(shape, dim):
    return lax.broadcasted_iota(jnp.int32, shape, dim)


def dot(a, b):
    return jnp.dot(a, b, preferred_element_type=F32)


def dot_nt(a, b):
    return lax.dot_general(a, b, (((1,), (1,)), ((), ())), preferred_element_type=F32)


def lanes(block, size=D):
    return pl.ds(pl.multiple_of(block * D, D), size)


def rows_at(start, size, unit=16):
    return pl.ds(pl.multiple_of(start, unit), size)


class Wires:
    def __init__(self, send, recv, here):
        self.send, self.recv, self.here = send, recv, here
        self.count = 0
        self.open = []

    def start(self, src, dst, to):
        n = self.count
        self.count += 1
        copy = pltpu.make_async_remote_copy(
            src_ref=src, dst_ref=dst, send_sem=self.send.at[n], recv_sem=self.recv.at[n],
            device_id=to, device_id_type=MESH,
        )
        copy.start()
        self.open.append(copy)
        return n

    def arrived(self, n, landed):
        pltpu.make_async_remote_copy(
            src_ref=landed, dst_ref=landed, send_sem=self.send.at[n], recv_sem=self.recv.at[n],
            device_id=self.here, device_id_type=MESH,
        ).wait_recv()

    def drain(self):
        for copy in self.open:
            copy.wait_send()


def kernel(
    tok_h, q1_h, q2_h, tea_h, len_ref, cnt_ref, w_h, head_h,
    rows_out, kv_out, head_out,
    tok, q1, q2, tea, w_full, head_full, kv, probs, probs_b, hidden, grad_h, grad_o, normed_b,
    tok_tx, tok_ty, norm_ty, tok_x_all, tok_y_all, norm_y_all, keys_all, vals_all, grad_rows, pack, unpack,
    part_x, part_y, y_in, x_in, z_out, z_in, kv_sum,
    send_sem, recv_sem, local_sem,
):
    g, f = lax.axis_index("dp"), lax.axis_index("fsdp")
    z, lo = g // 2, g % 2
    hi, x, c = f // 8, (f // 2) % 4, f % 2

    def at(z_, lo_, hi_, x_, c_):
        return (z_ * 2 + lo_, hi_ * 8 + x_ * 2 + c_)

    def xk(k):
        return (x + k) % 4

    def zk(k):
        return (z + k) % Z

    def yk(k):
        y_ = (hi * 2 + lo + k) % 4
        return y_ // 2, y_ % 2

    other = at(z, lo, hi, x, 1 - c)
    y_far = at(z, 1 - lo, 1 - hi, x, c)
    y_pair = at(z, 1 - lo, hi, x, c)
    y_two = at(z, lo, 1 - hi, x, c)

    loads = []
    for n, (src, dst) in enumerate(((tok_h, tok), (q1_h, q1), (q2_h, q2), (tea_h, tea))):
        load = pltpu.make_async_copy(src, dst, local_sem.at[n])
        load.start()
        loads.append(load)
    own_rows = rows_at(f * SHARD, SHARD)
    for n, (src, dst) in enumerate(((w_h, w_full), (head_h, head_full))):
        load = pltpu.make_async_copy(src, dst.at[own_rows], local_sem.at[4 + n])
        load.start()
        loads.append(load)

    peers = [other, y_far, y_two, at(z, 1 - lo, 1 - hi, x, 1 - c), at(z, 1 - lo, hi, x, 1 - c), at(z, lo, 1 - hi, x, 1 - c)]
    for k in (1, 2, 3):
        peers += [at(z, lo, hi, xk(k), c), at(z, lo, hi, xk(k), 1 - c)]
    for k in range(16):
        if k:
            peers.append(((g + k) % 16, f))
    barrier = pltpu.get_barrier_semaphore()
    for peer in peers:
        pl.semaphore_signal(barrier, inc=1, device_id=peer, device_id_type=MESH)
    pl.semaphore_wait(barrier, len(peers))

    wires = Wires(send_sem, recv_sem, other)

    def shard(full, hi_, x_, c_):
        return full.at[rows_at((hi_ * 8 + x_ * 2 + c_) * SHARD, SHARD)]

    def half(full, hi_, x_, c_, lo_):
        return full.at[rows_at((hi_ * 8 + x_ * 2 + c_) * SHARD + lo_ * HALF, HALF)]

    order = (0, 1, 3, 2)

    def gather_x(source, full):
        own = full.at[own_rows]
        n_x = {k: wires.start(source, own, at(z, lo, hi, xk(k), c)) for k in (1, 3, 2)}
        return n_x

    def gather_far(own_loaded, full, n_x):
        n_far, n_core = {}, []
        own_loaded.wait()
        for k in order:
            if k:
                wires.arrived(n_x[k], shard(full, hi, xk(4 - k), c))
            src = half(full, hi, xk(4 - k), c, 1 - lo)
            n_far[k] = wires.start(src, src, y_far)
            src = shard(full, hi, xk(4 - k), c)
            n_core.append((wires.start(src, src, other), shard(full, hi, xk(4 - k), 1 - c)))
        return n_far, n_core

    def gather_pair(full, n_far, n_core):
        n_pair = {}
        for k in order:
            src = half(full, 1 - hi, xk(4 - k), c, lo)
            wires.arrived(n_far[k], src)
            n_pair[k] = wires.start(src, src, y_pair)
            n_core.append((wires.start(src, src, other), half(full, 1 - hi, xk(4 - k), 1 - c, lo)))
        return n_pair

    def gather_core(full, n_pair, n_core):
        for k in order:
            src = half(full, 1 - hi, xk(4 - k), c, 1 - lo)
            wires.arrived(n_pair[k], src)
            n_core.append((wires.start(src, src, other), half(full, 1 - hi, xk(4 - k), 1 - c, 1 - lo)))

    kept = pl.ds(pl.multiple_of(z % 2 * (KV // 2), KV // 2), KV // 2)
    given = pl.ds(pl.multiple_of((1 - z % 2) * (KV // 2), KV // 2), KV // 2)

    def block(hi_, x_, c_, cols, half_=None):
        start = (hi_ * 8 + x_ * 2 + c_) * SHARD
        if half_ is None:
            return w_full.at[rows_at(start, SHARD), cols]
        return w_full.at[rows_at(start + half_ * HALF, HALF), cols]

    w_core, w_z = [], []

    def to_core(hi_, x_, cols, half_=None):
        src = block(hi_, x_, c, cols, half_)
        w_core.append((wires.start(src, src, other), block(hi_, x_, 1 - c, cols, half_)))

    def to_z(hi_, x_, half_):
        src = block(hi_, x_, c, kept, half_)
        n = wires.start(src, src, at((z + 1 - 2 * half_ + Z) % Z, lo, hi, x, c))
        w_z.append((n, hi_, x_, half_))

    def to_far(x_):
        src = block(hi, x_, c, kept, 1 - lo)
        return wires.start(src, src, y_far)

    loads[4].wait()
    n_x, n_far, n_pair = {}, {}, {}
    n_far[0] = to_far(x)

    def send_x(k, half_):
        src = block(hi, x, c, kept, half_)
        n_x.setdefault(k, []).append(wires.start(src, src, at(z, lo, hi, xk(k), c)))

    for half_ in (1 - lo, lo):
        send_x(1, half_)
        send_x(3, half_)
    to_core(hi, x, pl.ds(0, KV))
    loads[0].wait()

    def turn_rows(ref, m):
        blocks = [ref[:, lanes(5 * m + i)].T for i in range(5)]
        return jnp.concatenate(blocks, axis=0)

    def units(turned, m):
        for i in range(8):
            yield m // 2, m % 2 * 2 + i // 4, i // 2 % 2, i % 2, turned[i * HALF:(i + 1) * HALF, :]

    def y_order(h_, x_, c_, half_):
        return rows_at(((h_ * 2 + half_) * 2 + c_) * 2 * SHARD + x_ * HALF, HALF)

    def transpose_tokens(m, carry):
        for h_, x_, c_, half_, unit in units(turn_rows(tok, m), m):
            tok_tx[rows_at((x_ * 2 + c_) * 2 * SHARD + h_ * SHARD + half_ * HALF, HALF), :] = unit
            tok_ty[y_order(h_, x_, c_, half_), :] = unit
        return carry

    lax.fori_loop(0, 4, transpose_tokens, 0)
    send_x(2, 1 - lo)
    send_x(2, lo)

    def got_x(k, turn):
        x_ = xk(4 - k)
        half_ = lo if turn else 1 - lo
        wires.arrived(n_x[k][turn], block(hi, x_, c, kept, half_))
        to_z(hi, x_, half_)
        if not turn:
            n_far[k] = to_far(x_)
        to_core(hi, x_, kept, half_)

    def got_far(k):
        x_ = xk(4 - k)
        src = block(1 - hi, x_, c, kept, lo)
        wires.arrived(n_far[k], src)
        n_pair[k] = wires.start(src, src, y_pair)
        to_z(1 - hi, x_, lo)
        to_core(1 - hi, x_, kept, lo)

    def got_pair(k):
        x_ = xk(4 - k)
        wires.arrived(n_pair[k], block(1 - hi, x_, c, kept, 1 - lo))
        to_z(1 - hi, x_, 1 - lo)
        to_core(1 - hi, x_, kept, 1 - lo)

    got_far(0)
    got_x(1, 0)
    got_x(3, 0)
    got_x(1, 1)
    got_x(3, 1)
    got_pair(0)
    n_hx = gather_x(head_h, head_full)
    got_far(1)
    got_far(3)
    got_x(2, 0)
    got_x(2, 1)
    got_pair(1)
    got_pair(3)
    got_far(2)

    lens = len_ref[:, 0, :].astype(F32)
    counts = cnt_ref[:, 0, :].astype(F32)
    len_row = len_ref[g].astype(F32)
    cnt_row = cnt_ref[g].astype(F32)

    def lane_sum(a):
        return jnp.sum(a, axis=1, keepdims=True)

    def row_sum(a):
        return jnp.sum(a, axis=0, keepdims=True)

    ends_col = lane_sum(jnp.where(iota((32, 32), 1) <= iota((32, 32), 0), len_row, 0.0))
    len_col = lane_sum(jnp.where(iota((32, 32), 1) == iota((32, 32), 0), len_row, 0.0))
    ends_row = row_sum(jnp.where(iota((32, 32), 0) <= iota((32, 32), 1), len_col, 0.0))
    seg_col = lane_sum(jnp.where(iota((ROWS, 32), 0).astype(F32) >= ends_row, 1.0, 0.0))
    seg_row = row_sum(jnp.where(iota((32, ROWS), 1).astype(F32) >= ends_col, 1.0, 0.0))
    visible = (seg_col == seg_row) & (iota((ROWS, ROWS), 0) <= iota((ROWS, ROWS), 1))
    bias = jnp.where(visible, 0.0, -1e30).astype(F32)

    start_col = lane_sum(jnp.where(iota((16, 16), 1) < iota((16, 16), 0), cnt_row, 0.0))
    stop_col = lane_sum(jnp.where(iota((16, 16), 1) <= iota((16, 16), 0), cnt_row, 0.0))
    k_row = iota((16, 32), 1).astype(F32)
    begin_col = lane_sum(jnp.where(k_row < start_col, len_row, 0.0))
    size_col = lane_sum(jnp.where(k_row < stop_col, len_row, 0.0)) - begin_col
    spread = jnp.where(iota((256, 16), 0) // 16 == iota((256, 16), 1), 1.0, 0.0)
    begin = lane_sum(jnp.where(spread > 0.0, row_sum(jnp.where(iota((16, 16), 0) == iota((16, 16), 1), begin_col, 0.0)), 0.0))
    size = lane_sum(jnp.where(spread > 0.0, row_sum(jnp.where(iota((16, 16), 0) == iota((16, 16), 1), size_col, 0.0)), 0.0))
    slot = (iota((256, ROWS), 0) % 16).astype(F32)
    row_id = iota((256, ROWS), 1).astype(F32)
    main = jnp.where((slot < 12.0) & (slot < size) & (row_id == begin + slot), 1.0, 0.0)
    pack_lhs = []
    for r in range(3):
        w = slot - (12.0 - 4.0 * r)
        rest = jnp.where((slot >= 12.0) & (w < size) & (row_id == begin + w), 1.0, 0.0)
        pack_lhs.append(jnp.concatenate([main, rest], axis=1).astype(BF16))

    start_in = lane_sum(jnp.where(iota((16, 16), 1) < g, counts, 0.0))
    stop_in = lane_sum(jnp.where(iota((16, 16), 1) <= g, counts, 0.0))
    size_in = lane_sum(jnp.where((k_row >= start_in) & (k_row < stop_in), lens, 0.0))
    group = iota((16, 256), 1) // 16
    size_row = row_sum(jnp.where(group == iota((16, 256), 0), size_in, 0.0))
    base_row = row_sum(jnp.where(iota((16, 256), 0) < group, size_in, 0.0))
    slot = (iota((ROWS, 256), 1) % 16).astype(F32)
    place = iota((ROWS, 256), 0).astype(F32)
    unpack_main = jnp.where((slot < 12.0) & (slot < size_row) & (place == base_row + slot), 1.0, 0.0).astype(BF16)
    unpack_rest = []
    for r in range(3):
        w = slot - (12.0 - 4.0 * r)
        unpack_rest.append(jnp.where((slot >= 12.0) & (w < size_row) & (place == base_row + w), 1.0, 0.0).astype(BF16))

    got_pair(2)
    n_hfar, n_hcore = gather_far(loads[5], head_full, n_hx)
    def on_ring(along_x, k, c_):
        if along_x:
            return at(z, lo, hi, xk(k), c_), xk(k) * 2 + c_
        hi_, lo_ = yk(k)
        return at(z, lo_, hi_, x, c_), (hi_ * 2 + lo_) * 2 + c_

    def exchange_t(mine, everyone, along_x):
        numbers = []
        spot = on_ring(along_x, 0, c)[1]
        for k, c_ in ((1, c), (3, c), (1, 1 - c), (3, 1 - c), (2, c), (2, 1 - c), (0, 1 - c)):
            to, p_to = on_ring(along_x, k, c_)
            p_from = on_ring(along_x, 4 - k, c_)[1]
            n = wires.start(mine.at[rows_at(p_to * 2 * SHARD, 2 * SHARD), :], everyone.at[:, lanes(spot)], to)
            numbers.append((n, everyone.at[:, lanes(p_from)]))
        everyone[:, lanes(spot)] = mine[rows_at(spot * 2 * SHARD, 2 * SHARD), :]
        return numbers

    n_tx = exchange_t(tok_tx, tok_x_all, True)
    n_ty = exchange_t(tok_ty, tok_y_all, False)

    n_hpair = None
    for i, (n, hi_, x_, half_) in enumerate(w_z):
        if i == 10:
            n_hpair = gather_pair(head_full, n_hfar, n_hcore)
        wires.arrived(n, block(hi_, x_, c, given, half_))
        to_core(hi_, x_, given, half_)
    for n, landed in w_core:
        wires.arrived(n, landed)

    def project(b, carry):
        cols = pl.ds(pl.multiple_of(b * 256, 256), 256)
        kv[:, cols] = dot(tok[...], w_full[:, cols]).astype(BF16)
        return carry

    lax.fori_loop(0, KV // 256, project, 0)

    loads[1].wait()
    loads[2].wait()

    def softmax_cols(scores):
        s = scores * (SCALE * LOG2E) + bias
        e = jnp.exp2(s - jnp.max(s, axis=0, keepdims=True))
        return e * (1.0 / jnp.sum(e, axis=0, keepdims=True))

    def attend(j, squares):
        keys = kv[:, lanes(j)]
        values = kv[:, lanes(KV_HEADS + j)]
        heads = [j * PER_KEY + i for i in range(PER_KEY)]
        scores = [(dot_nt(keys, q1[:, lanes(h)]), dot_nt(keys, q2[:, lanes(h)])) for h in heads]
        turned = []
        for h, (s_one, s_two) in zip(heads, scores):
            one, two = softmax_cols(s_one), softmax_cols(s_two)
            probs[2 * h] = one
            probs[2 * h + 1] = two
            both = (one + two).astype(BF16)
            probs_b[h] = both
            turned.append(both.T)
        for h, both_t in zip(heads, turned):
            hid = tok[:, lanes(h)].astype(F32) + dot(both_t, values)
            hidden[:, lanes(h)] = hid
            squares = squares + hid * hid
        return squares

    squares = lax.fori_loop(0, 2, attend, jnp.zeros((ROWS, D), F32))
    gather_core(head_full, n_hpair, n_hcore)
    squares = lax.fori_loop(2, 4, attend, squares)
    inverse = lax.rsqrt(jnp.sum(squares, axis=1, keepdims=True) * (1.0 / WIDTH) + EPS)

    def normalise(m, carry):
        cols = pl.ds(pl.multiple_of(m * 640, 640), 640)
        normed_b[:, cols] = (hidden[:, cols] * inverse).astype(BF16)
        for h_, x_, c_, half_, unit in units(turn_rows(normed_b, m), m):
            norm_ty[y_order(h_, x_, c_, half_), :] = unit
        return carry

    lax.fori_loop(0, 4, normalise, 0)
    n_norm = exchange_t(norm_ty, norm_y_all, False)
    for n, landed in n_hcore:
        wires.arrived(n, landed)
    loads[3].wait()

    def softmax_rows(a):
        e = jnp.exp(a - jnp.max(a, axis=1, keepdims=True))
        return e / jnp.sum(e, axis=1, keepdims=True)

    student = softmax_rows(dot(normed_b[...], head_full[...]))
    grad_logits = (student - softmax_rows(tea[...].astype(F32))).astype(BF16)
    mine_x = rows_at(on_ring(True, 0, c)[1] * ROWS, ROWS, ROWS)
    mine_y = rows_at(on_ring(False, 0, c)[1] * ROWS, ROWS, ROWS)
    gl_cols = pl.ds(KV // 2, VOCAB)
    vals_all[mine_y, gl_cols] = grad_logits

    def ring_send(everyone, cols, along_x):
        src = everyone.at[rows_at(on_ring(along_x, 0, c)[1] * ROWS, ROWS, ROWS), cols]
        out = {k: wires.start(src, src, on_ring(along_x, k, c)[0]) for k in (1, 3, 2)}
        landed = everyone.at[rows_at(on_ring(along_x, 0, 1 - c)[1] * ROWS, ROWS, ROWS), cols]
        return out, [(wires.start(src, src, other), landed)]

    def ring_relay(everyone, cols, along_x, out, core):
        for k in (1, 3, 2):
            src = everyone.at[rows_at(on_ring(along_x, 4 - k, c)[1] * ROWS, ROWS, ROWS), cols]
            wires.arrived(out[k], src)
            landed = everyone.at[rows_at(on_ring(along_x, 4 - k, 1 - c)[1] * ROWS, ROWS, ROWS), cols]
            core.append((wires.start(src, src, other), landed))

    def wait_all(numbers):
        for n, landed in numbers:
            wires.arrived(n, landed)

    def back_head(b, dots):
        cols = pl.ds(pl.multiple_of(b * 512, 512), 512)
        gn = dot_nt(grad_logits, head_full[cols, :])
        grad_h[:, cols] = gn
        prod = gn * (hidden[:, cols] * inverse)
        for q in range(4):
            dots = dots + prod[:, q * D:(q + 1) * D]
        return dots

    dots = lax.fori_loop(0, WIDTH // 512, back_head, jnp.zeros((ROWS, D), F32))
    mean = jnp.sum(dots, axis=1, keepdims=True) * (1.0 / WIDTH)

    def back_norm(b, carry):
        cols = pl.ds(pl.multiple_of(b * 512, 512), 512)
        gh = inverse * (grad_h[:, cols] - (hidden[:, cols] * inverse) * mean)
        grad_h[:, cols] = gh
        grad_o[:, cols] = gh.astype(BF16)
        return carry

    lax.fori_loop(0, WIDTH // 512, back_norm, 0)

    def attend_back(j, carry):
        values = kv[:, lanes(KV_HEADS + j)]
        gk = jnp.zeros((ROWS, D), F32)
        gv = jnp.zeros((ROWS, D), F32)
        for i in range(PER_KEY):
            h = j * PER_KEY + i
            go = grad_o[:, lanes(h)]
            gp = dot_nt(values, go)
            gv = gv + dot(probs_b[h], go)
            for layer, queries in enumerate((q1, q2)):
                pr = probs[2 * h + layer]
                along = jnp.sum(pr * gp, axis=0, keepdims=True)
                gs = (pr * (gp - along) * SCALE).astype(BF16)
                gk = gk + dot(gs, queries[:, lanes(h)])
        keys_all[mine_x, lanes(j)] = gk.astype(BF16)
        vals_all[mine_y, lanes(j)] = gv.astype(BF16)
        return carry

    lax.fori_loop(0, KV_HEADS, attend_back, 0)

    kv_cols = pl.ds(0, KV // 2)
    n_keys = ring_send(keys_all, kv_cols, True)
    n_vals = ring_send(vals_all, kv_cols, False)
    n_gl = ring_send(vals_all, gl_cols, False)

    def back_rows(b, carry):
        cols = pl.ds(pl.multiple_of(b * 512, 512), 512)
        back = dot_nt(keys_all[mine_x, :], w_full[cols, :KV // 2]) + dot_nt(vals_all[mine_y, kv_cols], w_full[cols, KV // 2:])
        grad_rows[:, cols] = (grad_h[:, cols] + back).astype(BF16)
        return carry

    lax.fori_loop(0, WIDTH // 512, back_rows, 0)
    for e in range(5):
        rest = grad_rows[:, (15 + e) * D:(16 + e) * D]
        for r in range(3):
            b = 3 * e + r
            both = jnp.concatenate([grad_rows[:, b * D:(b + 1) * D], rest], axis=0)
            pack[:, b * D:(b + 1) * D] = dot(pack_lhs[r], both).astype(BF16)
    n_rows = []
    for k in (8, 7, 9, 6, 10, 5, 11, 4, 12, 3, 13, 2, 14, 1, 15):
        n = wires.start(pack.at[rows_at((g + k) % 16 * 16, 16)], unpack.at[rows_at(g * 16, 16)], ((g + k) % 16, f))
        n_rows.append((n, unpack.at[rows_at((g + 16 - k) % 16 * 16, 16)]))
    unpack[rows_at(g * 16, 16), :] = pack[rows_at(g * 16, 16), :]

    n_y = []

    def scatter_x(cols):
        for k in (1, 3, 2):
            landed = x_in.at[k - 1, :, cols]
            n_y.append((wires.start(part_y.at[rows_at(xk(k) * HALF, HALF), cols], landed, on_ring(True, k, c)[0]), landed))

    ring_relay(keys_all, kv_cols, True, *n_keys)
    ring_relay(vals_all, kv_cols, False, *n_vals)
    wait_all(n_tx)
    wait_all(n_keys[1])
    part_x[...] = dot(tok_x_all[...], keys_all[...]).astype(BF16)
    for k in (1, 3, 2):
        hi_, lo_ = yk(k)
        n = wires.start(part_x.at[rows_at(hi_ * SHARD + lo_ * HALF, HALF), :], y_in.at[k - 1], on_ring(False, k, c)[0])
        n_y.append((n, y_in.at[k - 1]))
    wait_all(n_ty)
    wait_all(n_vals[1])
    part_y[:, kv_cols] = dot(tok_y_all[...], vals_all[:, kv_cols]).astype(BF16)
    scatter_x(kv_cols)
    ring_relay(vals_all, gl_cols, False, *n_gl)
    wait_all(n_norm)
    wait_all(n_gl[1])
    part_y[:, gl_cols] = dot(norm_y_all[...], vals_all[:, gl_cols]).astype(BF16)
    scatter_x(gl_cols)
    own_x = rows_at(hi * SHARD + lo * HALF, HALF)
    own_y = rows_at(x * HALF, HALF)

    wait_all(n_y)

    def add(own, parts, cols):
        total = own.astype(F32)
        for n in range(3):
            total = total + parts[n, :, cols].astype(F32)
        return total.astype(BF16)

    def add_ring(b, carry):
        z_out[b, :HALF, :] = add(part_x[own_x, lanes(b)], y_in, lanes(b))
        z_out[b + 4, :HALF, :] = add(part_y[own_y, lanes(b)], x_in, lanes(b))
        return carry

    lax.fori_loop(0, 4, add_ring, 0)
    for v in range(2):
        cols = slice(KV // 2 + v * D, KV // 2 + (v + 1) * D)
        total = add(part_y[own_y, cols], x_in, cols)
        for b in range(Z):
            rows = total[b * 16:(b + 1) * 16] if b < 5 else jnp.zeros((16, D), BF16)
            z_out[b, HALF + v * 16:HALF + (v + 1) * 16, :] = rows
    n_z = []
    for k in (4, 3, 5, 2, 6, 1, 7):
        n = wires.start(z_out.at[zk(k)], z_in.at[z], at(zk(k), lo, hi, x, c))
        n_z.append((n, z_in.at[zk(Z - k)]))
    z_in[z] = z_out[z]

    for n, landed in n_z:
        wires.arrived(n, landed)
    total = z_in[0].astype(F32)
    for n in range(1, Z):
        total = total + z_in[n].astype(F32)
    kv_sum[lo, z] = total.astype(BF16)
    n_zg, n_pair = {}, []
    for k in (4, 3, 5, 2, 6, 1, 7):
        n_zg[k] = wires.start(kv_sum.at[lo, z], kv_sum.at[lo, z], at(zk(k), lo, hi, x, c))
    n_pair.append((wires.start(kv_sum.at[lo, z], kv_sum.at[lo, z], y_pair), kv_sum.at[1 - lo, z]))

    for n, landed in n_rows:
        wires.arrived(n, landed)
    rows_out[:, :15 * D] = dot(unpack_main, unpack[...]).astype(BF16)
    for e in range(5):
        acc = dot(unpack_rest[0], unpack[:, 3 * e * D:(3 * e + 1) * D])
        for r in (1, 2):
            acc = acc + dot(unpack_rest[r], unpack[:, (3 * e + r) * D:(3 * e + r + 1) * D])
        rows_out[:, (15 + e) * D:(16 + e) * D] = acc.astype(BF16)

    for k in (1, 7, 2, 6, 3, 5, 4):
        src = kv_sum.at[lo, zk(Z - k)]
        wires.arrived(n_zg[k], src)
        n_pair.append((wires.start(src, src, y_pair), kv_sum.at[1 - lo, zk(Z - k)]))
    for n, landed in n_pair:
        wires.arrived(n, landed)
    for l in range(2):
        for b in range(Z):
            kv_out[l * HALF:(l + 1) * HALF, b * D:(b + 1) * D] = kv_sum[l, b, :HALF, :].astype(F32)
        for b in range(5):
            for v in range(2):
                rows = kv_sum[l, b, HALF + v * 16:HALF + (v + 1) * 16, :].astype(F32)
                head_out[l * HALF + b * 16:l * HALF + (b + 1) * 16, v * D:(v + 1) * D] = rows
    wires.drain()


def on_device(tokens_in, queries_first, queries_second, teacher_logits, rollout_lengths, send_counts, key_value_weight, head_slice):
    big = pl.BlockSpec(memory_space=pltpu.HBM)
    small = pl.BlockSpec(memory_space=pltpu.VMEM)

    def buf(*shape, dtype=BF16):
        return pltpu.VMEM(shape, dtype)

    return pl.pallas_call(
        kernel,
        out_shape=(
            jax.ShapeDtypeStruct((ROWS, WIDTH), BF16),
            jax.ShapeDtypeStruct((SHARD, KV), F32),
            jax.ShapeDtypeStruct((SHARD, VOCAB), F32),
        ),
        in_specs=[big, big, big, big, small, small, big, big],
        out_specs=(small, small, small),
        scratch_shapes=[
            buf(ROWS, WIDTH), buf(ROWS, WIDTH), buf(ROWS, WIDTH), buf(ROWS, VOCAB),
            buf(WIDTH, KV), buf(WIDTH, VOCAB), buf(ROWS, KV),
            buf(2 * HEADS, ROWS, D, dtype=F32), buf(HEADS, ROWS, D),
            buf(ROWS, WIDTH, dtype=F32), buf(ROWS, WIDTH, dtype=F32), buf(ROWS, WIDTH), buf(ROWS, WIDTH),
            buf(WIDTH, ROWS), buf(WIDTH, ROWS), buf(WIDTH, ROWS),
            buf(2 * SHARD, 8 * ROWS), buf(2 * SHARD, 8 * ROWS), buf(2 * SHARD, 8 * ROWS),
            buf(8 * ROWS, KV // 2), buf(8 * ROWS, KV // 2 + VOCAB), buf(ROWS, WIDTH),
            buf(256, 15 * D), buf(256, 15 * D),
            buf(2 * SHARD, KV // 2), buf(2 * SHARD, KV // 2 + VOCAB), buf(3, HALF, KV // 2), buf(3, HALF, KV // 2 + VOCAB),
            buf(Z, HALF + 32, D), buf(Z, HALF + 32, D), buf(2, Z, HALF + 32, D),
            pltpu.SemaphoreType.DMA((COPIES,)), pltpu.SemaphoreType.DMA((COPIES,)), pltpu.SemaphoreType.DMA((6,)),
        ],
        compiler_params=pltpu.CompilerParams(collective_id=0, has_side_effects=True, vmem_limit_bytes=60 * 2**20),
        name="pair_backward",
    )(tokens_in, queries_first, queries_second, teacher_logits, rollout_lengths, send_counts, key_value_weight, head_slice)


def solution(mesh):
    in_specs = (
        P(("dp", "fsdp"), None),
        P(("dp", "fsdp"), None),
        P(("dp", "fsdp"), None),
        P(("dp", "fsdp"), None),
        P(None, "fsdp", None),
        P(None, "fsdp", None),
        P("fsdp", None),
        P("fsdp", None),
    )
    out_specs = (P(("dp", "fsdp"), None), P("fsdp", None), P("fsdp", None))
    return jax.shard_map(on_device, mesh=mesh, in_specs=in_specs, out_specs=out_specs, check_vma=False)
```

```python
import functools

import jax
import jax.numpy as jnp
from jax import lax
from jax.experimental import pallas as pl
from jax.experimental.pallas import tpu as pltpu
from jax.sharding import PartitionSpec as P

ROWS = 128
WIDTH = 2560
HEADS = 20
KV_HEADS = 4
PER_KEY = 5
D = 128
KV = 1024
VOCAB = 256
SHARD = 160
HALF = 80
Z = 8
EPS = 1e-06
SCALE = D ** (-0.5)
LOG2E = 1.4426950408889634
MESH = pl.DeviceIdType.MESH
F32 = jnp.float32
BF16 = jnp.bfloat16
COPIES = 200


def iota(shape, dim):
    return lax.broadcasted_iota(jnp.int32, shape, dim)


def dot(a, b):
    return jnp.dot(a, b, preferred_element_type=F32)


def dot_nt(a, b):
    return lax.dot_general(a, b, (((1,), (1,)), ((), ())), preferred_element_type=F32)


def lanes(block, size=D):
    return pl.ds(pl.multiple_of(block * D, D), size)


def rows_at(start, size, unit=16):
    return pl.ds(pl.multiple_of(start, unit), size)


class Wires:
    def __init__(self, send, recv, here):
        self.send, self.recv, self.here = send, recv, here
        self.count = 0
        self.open = []

    def start(self, src, dst, to):
        n = self.count
        self.count += 1
        copy = pltpu.make_async_remote_copy(
            src_ref=src, dst_ref=dst, send_sem=self.send.at[n], recv_sem=self.recv.at[n],
            device_id=to, device_id_type=MESH,
        )
        copy.start()
        self.open.append(copy)
        return n

    def arrived(self, n, landed):
        pltpu.make_async_remote_copy(
            src_ref=landed, dst_ref=landed, send_sem=self.send.at[n], recv_sem=self.recv.at[n],
            device_id=self.here, device_id_type=MESH,
        ).wait_recv()

    def drain(self):
        for copy in self.open:
            copy.wait_send()


def kernel(
    tok_h, q1_h, q2_h, tea_h, len_ref, cnt_ref, w_h, head_h,
    rows_out, kv_out, head_out,
    tok, q1, q2, tea, w_full, head_full, kv, probs, probs_b, hidden, grad_h, grad_o, normed_b,
    tok_tx, tok_ty, norm_ty, tok_x_all, tok_y_all, norm_y_all, keys_all, vals_all, grad_rows, pack, unpack,
    part_x, part_y, y_in, x_in, z_out, z_in, kv_sum,
    send_sem, recv_sem, local_sem,
):
    g, f = lax.axis_index("dp"), lax.axis_index("fsdp")
    z, lo = g // 2, g % 2
    hi, x, c = f // 8, (f // 2) % 4, f % 2

    def at(z_, lo_, hi_, x_, c_):
        return (z_ * 2 + lo_, hi_ * 8 + x_ * 2 + c_)

    def xk(k):
        return (x + k) % 4

    def zk(k):
        return (z + k) % Z

    def yk(k):
        y_ = (hi * 2 + lo + k) % 4
        return y_ // 2, y_ % 2

    other = at(z, lo, hi, x, 1 - c)
    y_far = at(z, 1 - lo, 1 - hi, x, c)
    y_pair = at(z, 1 - lo, hi, x, c)
    y_two = at(z, lo, 1 - hi, x, c)

    loads = []
    for n, (src, dst) in enumerate(((tok_h, tok), (q1_h, q1), (q2_h, q2), (tea_h, tea))):
        load = pltpu.make_async_copy(src, dst, local_sem.at[n])
        load.start()
        loads.append(load)
    own_rows = rows_at(f * SHARD, SHARD)
    for n, (src, dst) in enumerate(((w_h, w_full), (head_h, head_full))):
        load = pltpu.make_async_copy(src, dst.at[own_rows], local_sem.at[4 + n])
        load.start()
        loads.append(load)

    peers = [other, y_far, y_two, at(z, 1 - lo, 1 - hi, x, 1 - c), at(z, 1 - lo, hi, x, 1 - c), at(z, lo, 1 - hi, x, 1 - c)]
    for k in (1, 2, 3):
        peers += [at(z, lo, hi, xk(k), c), at(z, lo, hi, xk(k), 1 - c)]
    for k in range(16):
        if k:
            peers.append(((g + k) % 16, f))
    barrier = pltpu.get_barrier_semaphore()
    for peer in peers:
        pl.semaphore_signal(barrier, inc=1, device_id=peer, device_id_type=MESH)
    pl.semaphore_wait(barrier, len(peers))

    wires = Wires(send_sem, recv_sem, other)

    def shard(full, hi_, x_, c_):
        return full.at[rows_at((hi_ * 8 + x_ * 2 + c_) * SHARD, SHARD)]

    def half(full, hi_, x_, c_, lo_):
        return full.at[rows_at((hi_ * 8 + x_ * 2 + c_) * SHARD + lo_ * HALF, HALF)]

    order = (0, 1, 3, 2)

    def gather_x(source, full):
        own = full.at[own_rows]
        n_x = {k: wires.start(source, own, at(z, lo, hi, xk(k), c)) for k in (1, 3, 2)}
        return n_x

    def gather_far(own_loaded, full, n_x):
        n_far, n_core = {}, []
        own_loaded.wait()
        for k in order:
            if k:
                wires.arrived(n_x[k], shard(full, hi, xk(4 - k), c))
            src = half(full, hi, xk(4 - k), c, 1 - lo)
            n_far[k] = wires.start(src, src, y_far)
            src = shard(full, hi, xk(4 - k), c)
            n_core.append((wires.start(src, src, other), shard(full, hi, xk(4 - k), 1 - c)))
        return n_far, n_core

    def gather_pair(full, n_far, n_core):
        n_pair = {}
        for k in order:
            src = half(full, 1 - hi, xk(4 - k), c, lo)
            wires.arrived(n_far[k], src)
            n_pair[k] = wires.start(src, src, y_pair)
            n_core.append((wires.start(src, src, other), half(full, 1 - hi, xk(4 - k), 1 - c, lo)))
        return n_pair

    def gather_core(full, n_pair, n_core):
        for k in order:
            src = half(full, 1 - hi, xk(4 - k), c, 1 - lo)
            wires.arrived(n_pair[k], src)
            n_core.append((wires.start(src, src, other), half(full, 1 - hi, xk(4 - k), 1 - c, 1 - lo)))

    kept = pl.ds(pl.multiple_of(z % 2 * (KV // 2), KV // 2), KV // 2)
    given = pl.ds(pl.multiple_of((1 - z % 2) * (KV // 2), KV // 2), KV // 2)

    def block(hi_, x_, c_, cols, half_=None):
        start = (hi_ * 8 + x_ * 2 + c_) * SHARD
        if half_ is None:
            return w_full.at[rows_at(start, SHARD), cols]
        return w_full.at[rows_at(start + half_ * HALF, HALF), cols]

    w_core, w_z = [], []

    def to_core(hi_, x_, cols, half_=None):
        src = block(hi_, x_, c, cols, half_)
        w_core.append((wires.start(src, src, other), block(hi_, x_, 1 - c, cols, half_)))

    def to_z(hi_, x_, half_):
        src = block(hi_, x_, c, kept, half_)
        n = wires.start(src, src, at((z + 1 - 2 * half_ + Z) % Z, lo, hi, x, c))
        w_z.append((n, hi_, x_, half_))

    def to_far(x_):
        src = block(hi, x_, c, kept, 1 - lo)
        return wires.start(src, src, y_far)

    loads[4].wait()
    n_x, n_far, n_pair = {}, {}, {}
    n_far[0] = to_far(x)

    def send_x(k, half_):
        src = block(hi, x, c, kept, half_)
        n_x.setdefault(k, []).append(wires.start(src, src, at(z, lo, hi, xk(k), c)))

    for half_ in (1 - lo, lo):
        send_x(1, half_)
        send_x(3, half_)
    to_core(hi, x, pl.ds(0, KV))
    loads[0].wait()

    def turn_rows(ref, m):
        blocks = [ref[:, lanes(5 * m + i)].T for i in range(5)]
        return jnp.concatenate(blocks, axis=0)

    def units(turned, m):
        for i in range(8):
            yield m // 2, m % 2 * 2 + i // 4, i // 2 % 2, i % 2, turned[i * HALF:(i + 1) * HALF, :]

    def y_order(h_, x_, c_, half_):
        return rows_at(((h_ * 2 + half_) * 2 + c_) * 2 * SHARD + x_ * HALF, HALF)

    def transpose_tokens(m, carry):
        for h_, x_, c_, half_, unit in units(turn_rows(tok, m), m):
            tok_tx[rows_at((x_ * 2 + c_) * 2 * SHARD + h_ * SHARD + half_ * HALF, HALF), :] = unit
            tok_ty[y_order(h_, x_, c_, half_), :] = unit
        return carry

    lax.fori_loop(0, 4, transpose_tokens, 0)
    send_x(2, 1 - lo)
    send_x(2, lo)

    def got_x(k, turn):
        x_ = xk(4 - k)
        half_ = lo if turn else 1 - lo
        wires.arrived(n_x[k][turn], block(hi, x_, c, kept, half_))
        to_z(hi, x_, half_)
        if not turn:
            n_far[k] = to_far(x_)
        to_core(hi, x_, kept, half_)

    def got_far(k):
        x_ = xk(4 - k)
        src = block(1 - hi, x_, c, kept, lo)
        wires.arrived(n_far[k], src)
        n_pair[k] = wires.start(src, src, y_pair)
        to_z(1 - hi, x_, lo)
        to_core(1 - hi, x_, kept, lo)

    def got_pair(k):
        x_ = xk(4 - k)
        wires.arrived(n_pair[k], block(1 - hi, x_, c, kept, 1 - lo))
        to_z(1 - hi, x_, 1 - lo)
        to_core(1 - hi, x_, kept, 1 - lo)

    got_far(0)
    got_x(1, 0)
    got_x(3, 0)
    got_x(1, 1)
    got_x(3, 1)
    got_pair(0)
    n_hx = gather_x(head_h, head_full)
    got_far(1)
    got_far(3)
    got_x(2, 0)
    got_x(2, 1)
    got_pair(1)
    got_pair(3)
    got_far(2)

    lens = len_ref[:, 0, :].astype(F32)
    counts = cnt_ref[:, 0, :].astype(F32)
    len_row = len_ref[g].astype(F32)
    cnt_row = cnt_ref[g].astype(F32)

    def lane_sum(a):
        return jnp.sum(a, axis=1, keepdims=True)

    def row_sum(a):
        return jnp.sum(a, axis=0, keepdims=True)

    ends_col = lane_sum(jnp.where(iota((32, 32), 1) <= iota((32, 32), 0), len_row, 0.0))
    len_col = lane_sum(jnp.where(iota((32, 32), 1) == iota((32, 32), 0), len_row, 0.0))
    ends_row = row_sum(jnp.where(iota((32, 32), 0) <= iota((32, 32), 1), len_col, 0.0))
    seg_col = lane_sum(jnp.where(iota((ROWS, 32), 0).astype(F32) >= ends_row, 1.0, 0.0))
    seg_row = row_sum(jnp.where(iota((32, ROWS), 1).astype(F32) >= ends_col, 1.0, 0.0))
    visible = (seg_col == seg_row) & (iota((ROWS, ROWS), 0) <= iota((ROWS, ROWS), 1))
    bias = jnp.where(visible, 0.0, -1e30).astype(F32)

    start_col = lane_sum(jnp.where(iota((16, 16), 1) < iota((16, 16), 0), cnt_row, 0.0))
    stop_col = lane_sum(jnp.where(iota((16, 16), 1) <= iota((16, 16), 0), cnt_row, 0.0))
    k_row = iota((16, 32), 1).astype(F32)
    begin_col = lane_sum(jnp.where(k_row < start_col, len_row, 0.0))
    size_col = lane_sum(jnp.where(k_row < stop_col, len_row, 0.0)) - begin_col
    spread = jnp.where(iota((256, 16), 0) // 16 == iota((256, 16), 1), 1.0, 0.0)
    begin = lane_sum(jnp.where(spread > 0.0, row_sum(jnp.where(iota((16, 16), 0) == iota((16, 16), 1), begin_col, 0.0)), 0.0))
    size = lane_sum(jnp.where(spread > 0.0, row_sum(jnp.where(iota((16, 16), 0) == iota((16, 16), 1), size_col, 0.0)), 0.0))
    slot = (iota((256, ROWS), 0) % 16).astype(F32)
    row_id = iota((256, ROWS), 1).astype(F32)
    main = jnp.where((slot < 12.0) & (slot < size) & (row_id == begin + slot), 1.0, 0.0)
    pack_lhs = []
    for r in range(3):
        w = slot - (12.0 - 4.0 * r)
        rest = jnp.where((slot >= 12.0) & (w < size) & (row_id == begin + w), 1.0, 0.0)
        pack_lhs.append(jnp.concatenate([main, rest], axis=1).astype(BF16))

    start_in = lane_sum(jnp.where(iota((16, 16), 1) < g, counts, 0.0))
    stop_in = lane_sum(jnp.where(iota((16, 16), 1) <= g, counts, 0.0))
    size_in = lane_sum(jnp.where((k_row >= start_in) & (k_row < stop_in), lens, 0.0))
    group = iota((16, 256), 1) // 16
    size_row = row_sum(jnp.where(group == iota((16, 256), 0), size_in, 0.0))
    base_row = row_sum(jnp.where(iota((16, 256), 0) < group, size_in, 0.0))
    slot = (iota((ROWS, 256), 1) % 16).astype(F32)
    place = iota((ROWS, 256), 0).astype(F32)
    unpack_main = jnp.where((slot < 12.0) & (slot < size_row) & (place == base_row + slot), 1.0, 0.0).astype(BF16)
    unpack_rest = []
    for r in range(3):
        w = slot - (12.0 - 4.0 * r)
        unpack_rest.append(jnp.where((slot >= 12.0) & (w < size_row) & (place == base_row + w), 1.0, 0.0).astype(BF16))

    got_pair(2)
    n_hfar, n_hcore = gather_far(loads[5], head_full, n_hx)
    def on_ring(along_x, k, c_):
        if along_x:
            return at(z, lo, hi, xk(k), c_), xk(k) * 2 + c_
        hi_, lo_ = yk(k)
        return at(z, lo_, hi_, x, c_), (hi_ * 2 + lo_) * 2 + c_

    def exchange_t(mine, everyone, along_x):
        numbers = []
        spot = on_ring(along_x, 0, c)[1]
        for k, c_ in ((1, c), (3, c), (1, 1 - c), (3, 1 - c), (2, c), (2, 1 - c), (0, 1 - c)):
            to, p_to = on_ring(along_x, k, c_)
            p_from = on_ring(along_x, 4 - k, c_)[1]
            n = wires.start(mine.at[rows_at(p_to * 2 * SHARD, 2 * SHARD), :], everyone.at[:, lanes(spot)], to)
            numbers.append((n, everyone.at[:, lanes(p_from)]))
        everyone[:, lanes(spot)] = mine[rows_at(spot * 2 * SHARD, 2 * SHARD), :]
        return numbers

    n_tx = exchange_t(tok_tx, tok_x_all, True)
    n_ty = exchange_t(tok_ty, tok_y_all, False)

    n_hpair = None
    for i, (n, hi_, x_, half_) in enumerate(w_z):
        if i == 10:
            n_hpair = gather_pair(head_full, n_hfar, n_hcore)
        wires.arrived(n, block(hi_, x_, c, given, half_))
        to_core(hi_, x_, given, half_)
    for n, landed in w_core:
        wires.arrived(n, landed)

    def project(b, carry):
        cols = pl.ds(pl.multiple_of(b * 256, 256), 256)
        kv[:, cols] = dot(tok[...], w_full[:, cols]).astype(BF16)
        return carry

    lax.fori_loop(0, KV // 256, project, 0)

    loads[1].wait()
    loads[2].wait()

    def softmax_cols(scores):
        s = scores * (SCALE * LOG2E) + bias
        e = jnp.exp2(s - jnp.max(s, axis=0, keepdims=True))
        return e * (1.0 / jnp.sum(e, axis=0, keepdims=True))

    def attend(j, squares):
        keys = kv[:, lanes(j)]
        values = kv[:, lanes(KV_HEADS + j)]
        heads = [j * PER_KEY + i for i in range(PER_KEY)]
        scores = [(dot_nt(keys, q1[:, lanes(h)]), dot_nt(keys, q2[:, lanes(h)])) for h in heads]
        turned = []
        for h, (s_one, s_two) in zip(heads, scores):
            one, two = softmax_cols(s_one), softmax_cols(s_two)
            probs[2 * h] = one
            probs[2 * h + 1] = two
            both = (one + two).astype(BF16)
            probs_b[h] = both
            turned.append(both.T)
        for h, both_t in zip(heads, turned):
            hid = tok[:, lanes(h)].astype(F32) + dot(both_t, values)
            hidden[:, lanes(h)] = hid
            squares = squares + hid * hid
        return squares

    squares = lax.fori_loop(0, 2, attend, jnp.zeros((ROWS, D), F32))
    gather_core(head_full, n_hpair, n_hcore)
    squares = lax.fori_loop(2, 4, attend, squares)
    inverse = lax.rsqrt(jnp.sum(squares, axis=1, keepdims=True) * (1.0 / WIDTH) + EPS)

    def normalise(m, carry):
        cols = pl.ds(pl.multiple_of(m * 640, 640), 640)
        normed_b[:, cols] = (hidden[:, cols] * inverse).astype(BF16)
        for h_, x_, c_, half_, unit in units(turn_rows(normed_b, m), m):
            norm_ty[y_order(h_, x_, c_, half_), :] = unit
        return carry

    lax.fori_loop(0, 4, normalise, 0)
    n_norm = exchange_t(norm_ty, norm_y_all, False)
    for n, landed in n_hcore:
        wires.arrived(n, landed)
    loads[3].wait()

    def softmax_rows(a):
        e = jnp.exp(a - jnp.max(a, axis=1, keepdims=True))
        return e / jnp.sum(e, axis=1, keepdims=True)

    student = softmax_rows(dot(normed_b[...], head_full[...]))
    grad_logits = (student - softmax_rows(tea[...].astype(F32))).astype(BF16)
    mine_x = rows_at(on_ring(True, 0, c)[1] * ROWS, ROWS, ROWS)
    mine_y = rows_at(on_ring(False, 0, c)[1] * ROWS, ROWS, ROWS)
    gl_cols = pl.ds(KV // 2, VOCAB)
    vals_all[mine_y, gl_cols] = grad_logits

    def ring_send(everyone, cols, along_x):
        src = everyone.at[rows_at(on_ring(along_x, 0, c)[1] * ROWS, ROWS, ROWS), cols]
        out = {k: wires.start(src, src, on_ring(along_x, k, c)[0]) for k in (1, 3, 2)}
        landed = everyone.at[rows_at(on_ring(along_x, 0, 1 - c)[1] * ROWS, ROWS, ROWS), cols]
        return out, [(wires.start(src, src, other), landed)]

    def ring_relay(everyone, cols, along_x, out, core):
        for k in (1, 3, 2):
            src = everyone.at[rows_at(on_ring(along_x, 4 - k, c)[1] * ROWS, ROWS, ROWS), cols]
            wires.arrived(out[k], src)
            landed = everyone.at[rows_at(on_ring(along_x, 4 - k, 1 - c)[1] * ROWS, ROWS, ROWS), cols]
            core.append((wires.start(src, src, other), landed))

    def wait_all(numbers):
        for n, landed in numbers:
            wires.arrived(n, landed)

    def back_head(b, dots):
        cols = pl.ds(pl.multiple_of(b * 512, 512), 512)
        gn = dot_nt(grad_logits, head_full[cols, :])
        grad_h[:, cols] = gn
        prod = gn * (hidden[:, cols] * inverse)
        for q in range(4):
            dots = dots + prod[:, q * D:(q + 1) * D]
        return dots

    dots = lax.fori_loop(0, WIDTH // 512, back_head, jnp.zeros((ROWS, D), F32))
    mean = jnp.sum(dots, axis=1, keepdims=True) * (1.0 / WIDTH)

    def back_norm(b, carry):
        cols = pl.ds(pl.multiple_of(b * 512, 512), 512)
        gh = inverse * (grad_h[:, cols] - (hidden[:, cols] * inverse) * mean)
        grad_h[:, cols] = gh
        grad_o[:, cols] = gh.astype(BF16)
        return carry

    lax.fori_loop(0, WIDTH // 512, back_norm, 0)

    def attend_back(j, carry):
        values = kv[:, lanes(KV_HEADS + j)]
        gk = jnp.zeros((ROWS, D), F32)
        gv = jnp.zeros((ROWS, D), F32)
        heads = [j * PER_KEY + i for i in range(PER_KEY)]
        grad_probs = [dot_nt(values, grad_o[:, lanes(h)]) for h in heads]
        scores = []
        for h, gp in zip(heads, grad_probs):
            for layer in range(2):
                pr = probs[2 * h + layer]
                along = jnp.sum(pr * gp, axis=0, keepdims=True)
                scores.append((pr * (gp - along) * SCALE).astype(BF16))
        for i, h in enumerate(heads):
            gv = gv + dot(probs_b[h], grad_o[:, lanes(h)])
            gk = gk + dot(scores[2 * i], q1[:, lanes(h)]) + dot(scores[2 * i + 1], q2[:, lanes(h)])
        keys_all[mine_x, lanes(j)] = gk.astype(BF16)
        vals_all[mine_y, lanes(j)] = gv.astype(BF16)
        return carry

    lax.fori_loop(0, KV_HEADS, attend_back, 0)

    kv_cols = pl.ds(0, KV // 2)
    n_keys = ring_send(keys_all, kv_cols, True)
    n_vals = ring_send(vals_all, kv_cols, False)
    n_gl = ring_send(vals_all, gl_cols, False)

    def back_rows(b, carry):
        cols = pl.ds(pl.multiple_of(b * 512, 512), 512)
        back = dot_nt(keys_all[mine_x, :], w_full[cols, :KV // 2]) + dot_nt(vals_all[mine_y, kv_cols], w_full[cols, KV // 2:])
        grad_rows[:, cols] = (grad_h[:, cols] + back).astype(BF16)
        return carry

    lax.fori_loop(0, WIDTH // 512, back_rows, 0)
    for e in range(5):
        rest = grad_rows[:, (15 + e) * D:(16 + e) * D]
        for r in range(3):
            b = 3 * e + r
            both = jnp.concatenate([grad_rows[:, b * D:(b + 1) * D], rest], axis=0)
            pack[:, b * D:(b + 1) * D] = dot(pack_lhs[r], both).astype(BF16)
    n_rows = []
    for k in (8, 7, 9, 6, 10, 5, 11, 4, 12, 3, 13, 2, 14, 1, 15):
        n = wires.start(pack.at[rows_at((g + k) % 16 * 16, 16)], unpack.at[rows_at(g * 16, 16)], ((g + k) % 16, f))
        n_rows.append((n, unpack.at[rows_at((g + 16 - k) % 16 * 16, 16)]))
    unpack[rows_at(g * 16, 16), :] = pack[rows_at(g * 16, 16), :]

    n_y = []

    def scatter_x(cols):
        for k in (1, 3, 2):
            landed = x_in.at[k - 1, :, cols]
            n_y.append((wires.start(part_y.at[rows_at(xk(k) * HALF, HALF), cols], landed, on_ring(True, k, c)[0]), landed))

    ring_relay(keys_all, kv_cols, True, *n_keys)
    ring_relay(vals_all, kv_cols, False, *n_vals)
    wait_all(n_tx)
    wait_all(n_keys[1])
    part_x[...] = dot(tok_x_all[...], keys_all[...]).astype(BF16)
    for k in (1, 3, 2):
        hi_, lo_ = yk(k)
        n = wires.start(part_x.at[rows_at(hi_ * SHARD + lo_ * HALF, HALF), :], y_in.at[k - 1], on_ring(False, k, c)[0])
        n_y.append((n, y_in.at[k - 1]))
    wait_all(n_ty)
    wait_all(n_vals[1])
    part_y[:, kv_cols] = dot(tok_y_all[...], vals_all[:, kv_cols]).astype(BF16)
    scatter_x(kv_cols)
    ring_relay(vals_all, gl_cols, False, *n_gl)
    wait_all(n_norm)
    wait_all(n_gl[1])
    part_y[:, gl_cols] = dot(norm_y_all[...], vals_all[:, gl_cols]).astype(BF16)
    scatter_x(gl_cols)
    own_x = rows_at(hi * SHARD + lo * HALF, HALF)
    own_y = rows_at(x * HALF, HALF)

    wait_all(n_y)

    def add(own, parts, cols):
        total = own.astype(F32)
        for n in range(3):
            total = total + parts[n, :, cols].astype(F32)
        return total.astype(BF16)

    def add_ring(b, carry):
        z_out[b, :HALF, :] = add(part_x[own_x, lanes(b)], y_in, lanes(b))
        z_out[b + 4, :HALF, :] = add(part_y[own_y, lanes(b)], x_in, lanes(b))
        return carry

    lax.fori_loop(0, 4, add_ring, 0)
    for v in range(2):
        cols = slice(KV // 2 + v * D, KV // 2 + (v + 1) * D)
        total = add(part_y[own_y, cols], x_in, cols)
        for b in range(Z):
            rows = total[b * 16:(b + 1) * 16] if b < 5 else jnp.zeros((16, D), BF16)
            z_out[b, HALF + v * 16:HALF + (v + 1) * 16, :] = rows
    n_z = []
    for k in (4, 3, 5, 2, 6, 1, 7):
        n = wires.start(z_out.at[zk(k)], z_in.at[z], at(zk(k), lo, hi, x, c))
        n_z.append((n, z_in.at[zk(Z - k)]))
    z_in[z] = z_out[z]

    for n, landed in n_z:
        wires.arrived(n, landed)
    total = z_in[0].astype(F32)
    for n in range(1, Z):
        total = total + z_in[n].astype(F32)
    kv_sum[lo, z] = total.astype(BF16)
    n_zg, n_pair = {}, []
    for k in (4, 3, 5, 2, 6, 1, 7):
        n_zg[k] = wires.start(kv_sum.at[lo, z], kv_sum.at[lo, z], at(zk(k), lo, hi, x, c))
    n_pair.append((wires.start(kv_sum.at[lo, z], kv_sum.at[lo, z], y_pair), kv_sum.at[1 - lo, z]))

    for n, landed in n_rows:
        wires.arrived(n, landed)
    rows_out[:, :15 * D] = dot(unpack_main, unpack[...]).astype(BF16)
    for e in range(5):
        acc = dot(unpack_rest[0], unpack[:, 3 * e * D:(3 * e + 1) * D])
        for r in (1, 2):
            acc = acc + dot(unpack_rest[r], unpack[:, (3 * e + r) * D:(3 * e + r + 1) * D])
        rows_out[:, (15 + e) * D:(16 + e) * D] = acc.astype(BF16)

    for k in (1, 7, 2, 6, 3, 5, 4):
        src = kv_sum.at[lo, zk(Z - k)]
        wires.arrived(n_zg[k], src)
        n_pair.append((wires.start(src, src, y_pair), kv_sum.at[1 - lo, zk(Z - k)]))
    for n, landed in n_pair:
        wires.arrived(n, landed)
    for l in range(2):
        for b in range(Z):
            kv_out[l * HALF:(l + 1) * HALF, b * D:(b + 1) * D] = kv_sum[l, b, :HALF, :].astype(F32)
        for b in range(5):
            for v in range(2):
                rows = kv_sum[l, b, HALF + v * 16:HALF + (v + 1) * 16, :].astype(F32)
                head_out[l * HALF + b * 16:l * HALF + (b + 1) * 16, v * D:(v + 1) * D] = rows
    wires.drain()


def on_device(tokens_in, queries_first, queries_second, teacher_logits, rollout_lengths, send_counts, key_value_weight, head_slice):
    big = pl.BlockSpec(memory_space=pltpu.HBM)
    small = pl.BlockSpec(memory_space=pltpu.VMEM)

    def buf(*shape, dtype=BF16):
        return pltpu.VMEM(shape, dtype)

    return pl.pallas_call(
        kernel,
        out_shape=(
            jax.ShapeDtypeStruct((ROWS, WIDTH), BF16),
            jax.ShapeDtypeStruct((SHARD, KV), F32),
            jax.ShapeDtypeStruct((SHARD, VOCAB), F32),
        ),
        in_specs=[big, big, big, big, small, small, big, big],
        out_specs=(small, small, small),
        scratch_shapes=[
            buf(ROWS, WIDTH), buf(ROWS, WIDTH), buf(ROWS, WIDTH), buf(ROWS, VOCAB),
            buf(WIDTH, KV), buf(WIDTH, VOCAB), buf(ROWS, KV),
            buf(2 * HEADS, ROWS, D, dtype=F32), buf(HEADS, ROWS, D),
            buf(ROWS, WIDTH, dtype=F32), buf(ROWS, WIDTH, dtype=F32), buf(ROWS, WIDTH), buf(ROWS, WIDTH),
            buf(WIDTH, ROWS), buf(WIDTH, ROWS), buf(WIDTH, ROWS),
            buf(2 * SHARD, 8 * ROWS), buf(2 * SHARD, 8 * ROWS), buf(2 * SHARD, 8 * ROWS),
            buf(8 * ROWS, KV // 2), buf(8 * ROWS, KV // 2 + VOCAB), buf(ROWS, WIDTH),
            buf(256, 15 * D), buf(256, 15 * D),
            buf(2 * SHARD, KV // 2), buf(2 * SHARD, KV // 2 + VOCAB), buf(3, HALF, KV // 2), buf(3, HALF, KV // 2 + VOCAB),
            buf(Z, HALF + 32, D), buf(Z, HALF + 32, D), buf(2, Z, HALF + 32, D),
            pltpu.SemaphoreType.DMA((COPIES,)), pltpu.SemaphoreType.DMA((COPIES,)), pltpu.SemaphoreType.DMA((6,)),
        ],
        compiler_params=pltpu.CompilerParams(collective_id=0, has_side_effects=True, vmem_limit_bytes=60 * 2**20),
        name="pair_backward",
    )(tokens_in, queries_first, queries_second, teacher_logits, rollout_lengths, send_counts, key_value_weight, head_slice)


def solution(mesh):
    in_specs = (
        P(("dp", "fsdp"), None),
        P(("dp", "fsdp"), None),
        P(("dp", "fsdp"), None),
        P(("dp", "fsdp"), None),
        P(None, "fsdp", None),
        P(None, "fsdp", None),
        P("fsdp", None),
        P("fsdp", None),
    )
    out_specs = (P(("dp", "fsdp"), None), P("fsdp", None), P("fsdp", None))
    return jax.shard_map(on_device, mesh=mesh, in_specs=in_specs, out_specs=out_specs, check_vma=False)
```
